256 devices in a mesh: batch: 8 (over y_lo, x), seq: 32 (over z, y_hi, core).
Axes of the slice: x: 4, y: 4 (y_hi: 2, y_lo: 2; y = y_hi * 2 + y_lo), z: 8, core: 2. Of those that a mesh axis runs over, the one named last changes fastest.
Arguments:
- inputs: bfloat16 [8, 65536, 512], P('batch', 'seq'), may hold values from -100 to 100
- dilated_tap_weight: bfloat16 [2, 3, 512, 256], replicated, may hold values from -0.15625 to 0.15625
- pointwise_weight: bfloat16 [2, 256, 512], replicated, may hold values from -0.375 to 0.375
- stream_norm_gain: float32 [2, 512], replicated, may hold values from 0.5 to 1.5
- stream_norm_bias: float32 [2, 512], replicated, may hold values from -3 to 3
- conv_norm_gain: float32 [2, 256], replicated, may hold values from 0.5 to 1.5
- conv_norm_bias: float32 [2, 256], replicated, may hold values from -3 to 3
Outputs:
- head_bins: float32 [8, 8, 64, 8192], P('batch', None, 'seq')
The draws below stay inside these ranges and needn't reach their ends.
All inputs are finite; a program needn't handle non-finite values.
Results may differ from the reference program's by a relative error of at most 0.00095.
Values may be sent and summed in bfloat16 or wider, within the bound.
No kernel may reach another device: no remote copies, remote signals or barrier semaphores. Data moves between devices by JAX's collectives and lax.ppermute only.
A program may use at most 64 MiB of HBM per device.

```python
import jax
import jax.numpy as jnp
from jax import lax

CH = 512
MID = 256
HEADS = 8
POOL = 8
FIRST_DILATION = 256
SECOND_DILATION = 512
HEAD_DIM = 64
LENGTH = 65536
SEQS = 8
BINS = 8192


def draw_inputs(key, part):
    key_base, key_rows, key_cols, key_offset, key_seqscale, key_seqshift, key_seqchan = jax.random.split(key, 7)
    position = jnp.arange(LENGTH, dtype=jnp.float32) / LENGTH
    rising = jnp.exp(jnp.log(3.0) * (position - 0.5))
    seq_shift = jax.random.uniform(key_seqshift, (SEQS, 1, 1), jnp.float32, -3.0, 3.0)
    base = jnp.clip(jax.random.normal(key_base, (SEQS, LENGTH, CH), jnp.float32), -4.0, 4.0)
    row_scale = jnp.exp(jax.random.uniform(key_rows, (SEQS, LENGTH, 1), jnp.float32, jnp.log(0.3), jnp.log(3.0)))
    offset = 0.5 * jax.random.normal(key_offset, (CH,), jnp.float32)
    seq_scale = jnp.exp(jax.random.uniform(key_seqscale, (SEQS, 1, 1), jnp.float32, jnp.log(0.4), jnp.log(1.0)))
    seq_chan = 0.5 * jnp.clip(jax.random.normal(key_seqchan, (SEQS, 1, CH), jnp.float32), -2.0, 2.0)
    col_scale = jnp.exp(jax.random.uniform(key_cols, (CH,), jnp.float32, jnp.log(0.4), jnp.log(4.0)))
    values = base * row_scale * seq_scale * rising[None, :, None] * col_scale + jnp.clip(offset, -4.0, 4.0) + seq_shift + seq_chan
    return values.astype(jnp.bfloat16)


def bell_draw(stream_key, extent, width, reach, kind=jnp.bfloat16):
    values = jax.random.normal(stream_key, extent, jnp.float32) * width
    return jnp.minimum(jnp.maximum(values, -reach), reach).astype(kind)


def setup_inputs(seed: int = 0) -> dict:
    seeds = jax.random.split(jax.random.key(seed), 8)
    return {
        "inputs": draw_inputs(jax.random.fold_in(seeds[7], 71), 0),
        "dilated_tap_weight": bell_draw(seeds[1], (2, 3, CH, MID), (3 * CH) ** -0.5, 0.15625),
        "pointwise_weight": bell_draw(seeds[2], (2, MID, CH), MID ** -0.5, 0.375),
        "stream_norm_gain": jnp.clip(jax.random.uniform(seeds[3], (2, CH), jnp.float32, 0.5, 1.5), 0.5, 1.5),
        "stream_norm_bias": bell_draw(seeds[4], (2, CH), 0.5, 3.0, jnp.float32),
        "conv_norm_gain": jnp.clip(jax.random.uniform(seeds[5], (2, MID), jnp.float32, 0.5, 1.5), 0.5, 1.5),
        "conv_norm_bias": bell_draw(seeds[6], (2, MID), 0.5, 3.0, jnp.float32),
    }


EPS = 1e-05

def norm_gelu(values, scale_gain, shift_bias):
    average = lax.optimization_barrier(jnp.mean(values, axis=(0, 1)))
    variance = lax.optimization_barrier(jnp.mean(jnp.square(values - average), axis=(0, 1)))
    factor = scale_gain * lax.rsqrt(variance + EPS)
    return jax.nn.gelu((values - average) * factor + shift_bias, approximate=False).astype(jnp.bfloat16)

def dilated_residual_unit(residual_flow, conv_taps, point_proj, in_gain, in_bias, mid_gain, mid_bias, dilation):
    gelu_activated = norm_gelu(residual_flow, in_gain, in_bias)
    edge_padded = jnp.pad(gelu_activated, ((0, 0), (dilation, dilation), (0, 0)))
    earlier = edge_padded[:, :LENGTH]
    following = edge_padded[:, 2 * dilation:]

    def tap_sum(pieces):
        first, centre, last = pieces
        total = jnp.dot(first, conv_taps[0], preferred_element_type=jnp.float32)
        total = total + jnp.dot(centre, conv_taps[1], preferred_element_type=jnp.float32)
        return total + jnp.dot(last, conv_taps[2], preferred_element_type=jnp.float32)
    mixture = lax.map(tap_sum, (earlier, gelu_activated, following))
    gated = norm_gelu(mixture, mid_gain, mid_bias)

    def project(flat_rows):
        return jnp.dot(flat_rows, point_proj, preferred_element_type=jnp.float32)
    return residual_flow + lax.map(project, gated)

def reference(inputs, dilated_tap_weight, pointwise_weight, stream_norm_gain, stream_norm_bias, conv_norm_gain, conv_norm_bias):
    residual_flow = inputs.astype(jnp.float32)
    residual_flow = dilated_residual_unit(residual_flow, dilated_tap_weight[0], pointwise_weight[0], stream_norm_gain[0], stream_norm_bias[0], conv_norm_gain[0], conv_norm_bias[0], FIRST_DILATION)
    residual_flow = dilated_residual_unit(residual_flow, dilated_tap_weight[1], pointwise_weight[1], stream_norm_gain[1], stream_norm_bias[1], conv_norm_gain[1], conv_norm_bias[1], SECOND_DILATION)
    pooled = residual_flow.reshape(SEQS, BINS, POOL, CH).mean(axis=2)
    return pooled.reshape(SEQS, BINS, HEADS, HEAD_DIM).transpose(0, 2, 3, 1)
```

```python
import jax
import jax.numpy as jnp
from jax import lax
from jax.sharding import Mesh, PartitionSpec as P

HEADS = 8
POOL = 8
EPS = 1e-05

NAMES = ("y_lo", "x", "z", "y_hi", "core")
SIZES = (2, 4, 8, 2, 2)
BATCH = ("y_lo", "x")
SEQ = ("z", "y_hi", "core")
STAGES = (("z", "core"), ("y_lo", "x", "y_hi"))


def padded(x, width):
    peers, length = (lax.axis_size(SEQ), x.shape[1])
    up = [(i, i + 1) for i in range(peers - 1)]
    down = [(j, i) for i, j in up]
    before = lax.ppermute(x[:, length - width :], SEQ, up)
    after = lax.ppermute(x[:, :width], SEQ, down)
    return jnp.concatenate([before, x, after], axis=1)


def moments(values):
    count = values.shape[0] * values.shape[1]
    mean = jnp.sum(values, axis=(0, 1)) / count
    deviation = values - mean
    stats = jnp.stack([mean, jnp.sum(deviation * deviation, axis=(0, 1))])
    for axes in STAGES:
        peers = lax.axis_size(axes)
        tiles = stats.reshape(-1, 128)
        sent = jnp.broadcast_to(tiles[None], (peers,) + tiles.shape)
        got = lax.all_to_all(sent, axes, 0, 0, tiled=True).reshape(peers, 2, -1)
        mean = jnp.mean(got[:, 0], axis=0)
        spread = got[:, 0] - mean
        stats = jnp.stack([mean, jnp.sum(got[:, 1], axis=0) + count * jnp.sum(spread * spread, axis=0)])
        count = count * peers
    return stats[0], stats[1] / count


def norm_gelu(values, gain, bias):
    average, variance = moments(values)
    factor = gain * lax.rsqrt(variance + EPS)
    return jax.nn.gelu((values - average) * factor + bias, approximate=False).astype(jnp.bfloat16)


def block(stream, taps, point, in_gain, in_bias, mid_gain, mid_bias, dilation):
    seqs, rows, channels = stream.shape
    edged = padded(norm_gelu(stream, in_gain, in_bias), dilation)

    def tap(k):
        piece = edged[:, k * dilation : k * dilation + rows].reshape(-1, channels)
        return jnp.dot(piece, taps[k], preferred_element_type=jnp.float32)

    mixture = (tap(1) + tap(0) + tap(2)).reshape(seqs, rows, -1)
    gated = norm_gelu(mixture, mid_gain, mid_bias)
    branch = jnp.dot(gated.reshape(seqs * rows, -1), point, preferred_element_type=jnp.float32)
    return stream + branch.reshape(stream.shape)


def per_device(inputs, taps, point, in_gain, in_bias, mid_gain, mid_bias):
    seqs, rows, channels = inputs.shape
    stream = inputs.astype(jnp.float32)
    for k, dilation in enumerate((256, 512)):
        stream = block(
            stream, taps[k], point[k], in_gain[k], in_bias[k], mid_gain[k], mid_bias[k], dilation
        )
    pooled = stream.reshape(seqs, rows // POOL, POOL, channels).mean(axis=2)
    grouped = pooled.reshape(seqs, rows // POOL, HEADS, channels // HEADS).transpose(0, 2, 3, 1)
    return lax.all_to_all(grouped, SEQ, split_axis=2, concat_axis=3, tiled=True)


def solution(mesh):
    fine = Mesh(mesh.devices.reshape(SIZES), NAMES)
    return jax.shard_map(
        per_device,
        mesh=fine,
        in_specs=(P(BATCH, SEQ, None), P(), P(), P(), P(), P(), P()),
        out_specs=P(BATCH, None, SEQ, None),
        check_vma=False,
    )
```

```python
import functools

import jax
import jax.numpy as jnp
from jax import lax
from jax.experimental import pallas as pl
from jax.experimental.pallas import tpu as pltpu
from jax.sharding import Mesh, PartitionSpec as P

EPS = 1e-05
HEADS = 8
POOL = 8
ROWS = 2048
CH = 512
MID = 256
TILE = 256
CHUNK = 32

NAMES = ("y_lo", "x", "z", "y_hi", "core")
SIZES = (2, 4, 8, 2, 2)
BATCH = ("y_lo", "x")
SEQ = ("z", "y_hi", "core")
STAGES = (("z", "core"), ("y_lo", "x", "y_hi"))
PEERS = 16
F32 = jnp.float32
BF16 = jnp.bfloat16


def gelu(u):
    return 0.5 * u * (1.0 + lax.erf(u * 0.7071067811865476))


def wide(v):
    return jnp.concatenate([v[j : j + 1] for j in range(v.shape[0])], axis=1)


def norm_terms(layer, got_ref, gain_ref, bias_ref):
    rows = got_ref.shape[1] // 2
    got = got_ref[...]
    means = got[:, :rows]
    mean = jnp.sum(means, axis=0) * (1.0 / PEERS)
    spread = means - mean
    total = jnp.sum(got[:, rows:], axis=0) + (PEERS * ROWS) * jnp.sum(spread * spread, axis=0)
    variance = wide(total) * (1.0 / (PEERS * PEERS * ROWS))
    return wide(mean), gain_ref[layer : layer + 1] * lax.rsqrt(variance + EPS), bias_ref[layer : layer + 1]


def fold(v):
    return jnp.sum(v.reshape(-1, 8, v.shape[-1]), axis=0)


def put_stats(out_ref, mean, squares):
    rows = out_ref.shape[1] // 2
    for j in range(rows):
        for base, v in ((0, mean), (rows, squares)):
            piece = v[:, 128 * j : 128 * (j + 1)].reshape(1, 1, 128)
            out_ref[:, base + j : base + j + 1, :] = jnp.broadcast_to(piece, (PEERS, 1, 128))


def row_slice(i, size):
    return pl.ds(pl.multiple_of(i * size, size), size)


def deviations(refs, mean, channels):
    squares = jnp.zeros((8, channels), F32)
    for ref in refs:

        def step(i, acc, ref=ref):
            d = ref[row_slice(i, 64), :].astype(F32) - mean
            return acc + fold(d * d)

        squares = lax.fori_loop(0, ref.shape[0] // 64, step, squares, unroll=4)
    return jnp.sum(squares, axis=0, keepdims=True)


def input_stats(x_ref, low_ref, high_ref, out_ref):
    low_ref[...] = x_ref[: low_ref.shape[0], :]
    high_ref[...] = x_ref[ROWS - high_ref.shape[0] :, :]

    def step(i, acc):
        return acc + fold(x_ref[row_slice(i, 64), :].astype(F32))

    acc = lax.fori_loop(0, ROWS // 64, step, jnp.zeros((8, CH), F32), unroll=4)
    mean = jnp.sum(acc, axis=0, keepdims=True) * (1.0 / ROWS)
    put_stats(out_ref, mean, deviations((x_ref,), mean, CH))


def conv_kernel(layer, dilation, sources, flag_ref, got_ref, gain_ref, bias_ref, taps_ref, *refs):
    pieces = refs[:sources]
    conv_ref, stats_ref, act_ref = refs[sources:]
    mean, factor, bias = norm_terms(layer, got_ref, gain_ref, bias_ref)
    start = 0
    for k, piece in enumerate(pieces):

        def step(i, carry, piece=piece, start=start, k=k):
            v = piece[row_slice(i, CHUNK), :].astype(F32)
            a = gelu((v - mean) * factor + bias)
            if k == 0:
                a = jnp.where(flag_ref[0] > 0, a, 0.0)
            if k == sources - 1:
                a = jnp.where(flag_ref[1] > 0, a, 0.0)
            act_ref[pl.ds(pl.multiple_of(start + i * CHUNK, CHUNK), CHUNK), :] = a.astype(BF16)
            return carry

        lax.fori_loop(0, piece.shape[0] // CHUNK, step, 0)
        start += piece.shape[0]

    def tile(i, acc):
        base = pl.multiple_of(i * TILE, TILE)
        total = jnp.dot(act_ref[pl.ds(base + dilation, TILE), :], taps_ref[layer, 1], preferred_element_type=F32)
        total += jnp.dot(act_ref[pl.ds(base, TILE), :], taps_ref[layer, 0], preferred_element_type=F32)
        total += jnp.dot(act_ref[pl.ds(base + 2 * dilation, TILE), :], taps_ref[layer, 2], preferred_element_type=F32)
        conv_ref[pl.ds(base, TILE), :] = total
        return acc + fold(total)

    acc = lax.fori_loop(0, ROWS // TILE, tile, jnp.zeros((8, MID), F32))
    mean = jnp.sum(acc, axis=0, keepdims=True) * (1.0 / ROWS)
    put_stats(stats_ref, mean, deviations((conv_ref,), mean, MID))


def gated_tile(conv_ref, i, terms, gated_ref):
    mean, factor, bias = terms
    for c in range(TILE // CHUNK):
        v = conv_ref[pl.ds(pl.multiple_of(i * TILE + c * CHUNK, CHUNK), CHUNK), :]
        gated_ref[c * CHUNK : (c + 1) * CHUNK, :] = gelu((v - mean) * factor + bias).astype(BF16)
    return gated_ref[...]


def point_kernel(
    layer, got_ref, gain_ref, bias_ref, point_ref, conv_ref, x_ref, low_ref, mid_ref, high_ref, stats_ref, pool_ref, gated_ref
):
    terms = norm_terms(layer, got_ref, gain_ref, bias_ref)
    acc = jnp.zeros((8, CH), F32)
    start = 0
    regions = (low_ref, mid_ref, high_ref)
    for region in regions:
        count = region.shape[0] // TILE

        def tile(i, acc, region=region, start=start):
            gated = gated_tile(conv_ref, start + i, terms, gated_ref)
            branch = jnp.dot(gated, point_ref[layer], preferred_element_type=F32)
            total = x_ref[row_slice(start + i, TILE), :].astype(F32) + branch
            region[row_slice(i, TILE), :] = total
            pool_ref[row_slice(start + i, TILE // POOL), :] = jnp.sum(
                total.reshape(TILE // POOL, POOL, CH), axis=1
            )
            return acc + fold(total)

        acc = lax.fori_loop(0, count, tile, acc)
        start += count
    mean = jnp.sum(acc, axis=0, keepdims=True) * (1.0 / ROWS)
    put_stats(stats_ref, mean, deviations(regions, mean, CH))


def pool_kernel(
    layer, got_ref, gain_ref, bias_ref, point_ref, conv_ref, pool_ref, out_ref, gated_ref, sums_ref, flip_ref
):
    terms = norm_terms(layer, got_ref, gain_ref, bias_ref)
    bins = TILE // POOL
    row = lax.broadcasted_iota(jnp.int32, (bins, TILE), 0)
    col = lax.broadcasted_iota(jnp.int32, (bins, TILE), 1)
    pick = jnp.where(col // POOL == row, 1.0, 0.0).astype(BF16)

    def tile(i, carry):
        gated = gated_tile(conv_ref, i, terms, gated_ref)
        sums_ref[row_slice(i, bins), :] = jnp.dot(pick, gated, preferred_element_type=F32)
        return carry

    lax.fori_loop(0, ROWS // TILE, tile, 0)
    sums = sums_ref[...]
    upper = sums.astype(BF16)
    lower = (sums - upper.astype(F32)).astype(BF16)
    branch = jnp.dot(upper, point_ref[layer], preferred_element_type=F32)
    branch += jnp.dot(lower, point_ref[layer], preferred_element_type=F32)
    flipped = ((pool_ref[...] + branch) * (1.0 / POOL)).T
    size = CH // HEADS
    for k in range(ROWS // POOL // 128):
        half = flip_ref.at[k]
        for h in range(HEADS):
            half[pl.ds(h, size, stride=HEADS), :] = flipped[h * size : (h + 1) * size, 128 * k : 128 * (k + 1)]
        out_ref[:, 128 * k : 128 * (k + 1)] = half[...]


VMEM = pl.BlockSpec(memory_space=pltpu.VMEM)
SMEM = pl.BlockSpec(memory_space=pltpu.SMEM)
PARAMS = pltpu.CompilerParams(vmem_limit_bytes=20 * 1024 * 1024)


def call(body, args, outs, scratch=(), scalars=0):
    return pl.pallas_call(
        body,
        out_shape=[jax.ShapeDtypeStruct(s, d) for s, d in outs],
        in_specs=[SMEM] * scalars + [VMEM] * (len(args) - scalars),
        out_specs=[VMEM] * len(outs),
        scratch_shapes=[pltpu.VMEM(s, d) for s, d in scratch],
        compiler_params=PARAMS,
    )(*args)


def reduce_stats(sent):
    got = lax.all_to_all(sent, STAGES[0], 0, 0, tiled=True)
    rows = got.shape[1] // 2
    means = got[:, :rows]
    mean = jnp.mean(means, axis=0)
    spread = means - mean
    squares = jnp.sum(got[:, rows:], axis=0) + ROWS * jnp.sum(spread * spread, axis=0)
    both = jnp.concatenate([mean, squares])
    return lax.all_to_all(jnp.broadcast_to(both[None], sent.shape), STAGES[1], 0, 0, tiled=True)


def halos(low, high):
    up = [(i, i + 1) for i in range(lax.axis_size(SEQ) - 1)]
    down = [(j, i) for i, j in up]
    return lax.ppermute(high, SEQ, up), lax.ppermute(low, SEQ, down)


def per_device(inputs, taps, point, in_gain, in_bias, mid_gain, mid_bias):
    place = lax.axis_index(SEQ)
    flags = jnp.stack([place > 0, place < lax.axis_size(SEQ) - 1]).astype(jnp.int32)
    x = inputs.reshape(ROWS, CH)
    wide_stats = ((PEERS, 8, 128), F32)
    slim_stats = ((PEERS, 4, 128), F32)
    conv_shape = ((ROWS, MID), F32)
    edge = ((512, CH), F32)

    thin = ((256, CH), BF16)
    low, high, stats = call(input_stats, (x,), [thin, thin, wide_stats])
    before, after = halos(low, high)
    got = reduce_stats(stats)
    conv, stats = call(
        functools.partial(conv_kernel, 0, 256, 3),
        (flags, got, in_gain, in_bias, taps, before, x, after),
        [conv_shape, slim_stats],
        [((ROWS + 512, CH), BF16)],
        1,
    )
    got = reduce_stats(stats)
    low, mid, high, stats, pooled = call(
        functools.partial(point_kernel, 0),
        (got, mid_gain, mid_bias, point, conv, x),
        [edge, ((1024, CH), F32), edge, wide_stats, ((ROWS // POOL, CH), F32)],
        [((TILE, MID), BF16)],
    )
    before, after = halos(low, high)
    got = reduce_stats(stats)
    conv, stats = call(
        functools.partial(conv_kernel, 1, 512, 5),
        (flags, got, in_gain, in_bias, taps, before, low, mid, high, after),
        [conv_shape, slim_stats],
        [((ROWS + 1024, CH), BF16)],
        1,
    )
    got = reduce_stats(stats)
    (out,) = call(
        functools.partial(pool_kernel, 1),
        (got, mid_gain, mid_bias, point, conv, pooled),
        [((CH, ROWS // POOL), F32)],
        [((TILE, MID), BF16), ((ROWS // POOL, MID), F32), ((ROWS // POOL // 128, CH, 128), F32)],
    )
    bins = ROWS // POOL
    out = lax.all_to_all(out.reshape(CH // HEADS, HEADS, bins), SEQ, 0, 0, tiled=True)
    peers = lax.axis_size(SEQ)
    out = out.reshape(peers, -1, HEADS, bins).transpose(2, 1, 0, 3)
    return out.reshape(1, HEADS, -1, peers * bins)


def solution(mesh):
    fine = Mesh(mesh.devices.reshape(SIZES), NAMES)
    return jax.shard_map(
        per_device,
        mesh=fine,
        in_specs=(P(BATCH, SEQ, None), P(), P(), P(), P(), P(), P()),
        out_specs=P(BATCH, None, SEQ, None),
        check_vma=False,
    )
```

```python
import functools

import jax
import jax.numpy as jnp
from jax import lax
from jax.experimental import pallas as pl
from jax.experimental.pallas import tpu as pltpu
from jax.sharding import Mesh, PartitionSpec as P

EPS = 1e-05
HEADS = 8
POOL = 8
ROWS = 2048
CH = 512
MID = 256
TILE = 256
CHUNK = 32
NEAR = 256
FAR = 512

NAMES = ("y_lo", "x", "z", "y_hi", "core")
SIZES = (2, 4, 8, 2, 2)
BATCH = ("y_lo", "x")
SEQ = ("z", "y_hi", "core")
ACROSS = ("y_lo", "x", "y_hi")
ALONG = ("z", "core")
PEERS = 16
F32 = jnp.float32
BF16 = jnp.bfloat16


def gelu(u):
    return 0.5 * u * (1.0 + lax.erf(u * 0.7071067811865476))


def wide(v):
    return jnp.concatenate([v[j : j + 1] for j in range(v.shape[0])], axis=1)


def norm_terms(layer, got_ref, gain_ref, bias_ref):
    rows = got_ref.shape[1] // 2
    got = got_ref[...]
    means = got[:, :rows]
    mean = jnp.sum(means, axis=0) * (1.0 / PEERS)
    spread = means - mean
    total = jnp.sum(got[:, rows:], axis=0) + (PEERS * ROWS) * jnp.sum(spread * spread, axis=0)
    variance = wide(total) * (1.0 / (PEERS * PEERS * ROWS))
    return wide(mean), gain_ref[layer : layer + 1] * lax.rsqrt(variance + EPS), bias_ref[layer : layer + 1]


def fold(v):
    return jnp.sum(v.reshape(-1, 8, v.shape[-1]), axis=0)


def put_stats(out_ref, mean, squares):
    rows = out_ref.shape[1] // 2
    for j in range(rows):
        for base, v in ((0, mean), (rows, squares)):
            piece = v[:, 128 * j : 128 * (j + 1)].reshape(1, 1, 128)
            out_ref[:, base + j : base + j + 1, :] = jnp.broadcast_to(piece, (PEERS, 1, 128))


def row_slice(i, size):
    return pl.ds(pl.multiple_of(i * size, size), size)


def deviations(refs, mean, channels):
    squares = jnp.zeros((8, channels), F32)
    for ref in refs:

        def step(i, acc, ref=ref):
            d = ref[row_slice(i, 64), :].astype(F32) - mean
            return acc + fold(d * d)

        squares = lax.fori_loop(0, ref.shape[0] // 64, step, squares, unroll=4)
    return jnp.sum(squares, axis=0, keepdims=True)


def input_stats(place_ref, x_ref, facing_ref, outer_ref, out_ref):
    put_edges(place_ref[0], x_ref, facing_ref, outer_ref)

    def step(i, acc):
        return acc + fold(x_ref[row_slice(i, 64), :].astype(F32))

    acc = lax.fori_loop(0, ROWS // 64, step, jnp.zeros((8, CH), F32), unroll=4)
    mean = jnp.sum(acc, axis=0, keepdims=True) * (1.0 / ROWS)
    put_stats(out_ref, mean, deviations((x_ref,), mean, CH))


def activate(piece, first, count, terms, act_ref, offset, flag=None):
    mean, factor, bias = terms

    def step(i, carry):
        v = piece[pl.ds(pl.multiple_of(first + i * CHUNK, CHUNK), CHUNK), :].astype(F32)
        a = gelu((v - mean) * factor + bias)
        if flag is not None:
            a = jnp.where(flag > 0, a, 0.0)
        act_ref[pl.ds(pl.multiple_of(offset + i * CHUNK, CHUNK), CHUNK), :] = a.astype(BF16)
        return carry

    lax.fori_loop(0, count // CHUNK, step, 0)


def convolve(layer, dilation, act_ref, taps_ref, conv_ref, first, count, acc):
    def tile(i, acc):
        base = pl.multiple_of(first + i * TILE, TILE)
        total = jnp.dot(act_ref[pl.ds(base + dilation, TILE), :], taps_ref[layer, 1], preferred_element_type=F32)
        total += jnp.dot(act_ref[pl.ds(base, TILE), :], taps_ref[layer, 0], preferred_element_type=F32)
        total += jnp.dot(act_ref[pl.ds(base + 2 * dilation, TILE), :], taps_ref[layer, 2], preferred_element_type=F32)
        conv_ref[pl.ds(base, TILE), :] = total
        return acc + fold(total)

    return lax.fori_loop(0, count // TILE, tile, acc)


def conv_stats(acc, center, stats_ref):
    mean = jnp.sum(acc, axis=0, keepdims=True) * (1.0 / ROWS)
    put_stats(stats_ref, mean, deviations((center,), mean, MID))


def conv_kernel(
    layer,
    dilation,
    place_ref,
    got_ref,
    gain_ref,
    bias_ref,
    taps_ref,
    near_ref,
    center_ref,
    cross_ref,
    conv_ref,
    stats_ref,
    act_ref,
):
    terms = norm_terms(layer, got_ref, gain_ref, bias_ref)
    core = place_ref[0]
    activate(near_ref, 0, dilation, terms, act_ref, (1 - core) * (dilation + ROWS))
    activate(center_ref, 0, ROWS, terms, act_ref, dilation)
    activate(cross_ref, 0, dilation, terms, act_ref, core * (dilation + ROWS), place_ref[1])
    acc = convolve(layer, dilation, act_ref, taps_ref, conv_ref, 0, ROWS, jnp.zeros((8, MID), F32))
    conv_stats(acc, conv_ref, stats_ref)


def put_edges(core, rows_ref, facing_ref, outer_ref):
    size = facing_ref.shape[0]
    last = ROWS - size
    facing_ref[...] = rows_ref[pl.ds(pl.multiple_of((1 - core) * last, 256), size), :]
    outer_ref[...] = rows_ref[pl.ds(pl.multiple_of(core * last, 256), size), :]


def gated_tile(conv_ref, i, terms, gated_ref):
    mean, factor, bias = terms
    for c in range(TILE // CHUNK):
        v = conv_ref[pl.ds(pl.multiple_of(i * TILE + c * CHUNK, CHUNK), CHUNK), :]
        gated_ref[c * CHUNK : (c + 1) * CHUNK, :] = gelu((v - mean) * factor + bias).astype(BF16)
    return gated_ref[...]


def point_kernel(
    place_ref,
    got_ref,
    gain_ref,
    bias_ref,
    point_ref,
    conv_ref,
    x_ref,
    stream_ref,
    facing_ref,
    outer_ref,
    stats_ref,
    pool_ref,
    gated_ref,
):
    terms = norm_terms(0, got_ref, gain_ref, bias_ref)

    def tile(i, acc):
        gated = gated_tile(conv_ref, i, terms, gated_ref)
        branch = jnp.dot(gated, point_ref[0], preferred_element_type=F32)
        total = x_ref[row_slice(i, TILE), :].astype(F32) + branch
        stream_ref[row_slice(i, TILE), :] = total
        pool_ref[row_slice(i, TILE // POOL), :] = jnp.sum(total.reshape(TILE // POOL, POOL, CH), axis=1)
        return acc + fold(total)

    acc = lax.fori_loop(0, ROWS // TILE, tile, jnp.zeros((8, CH), F32))
    put_edges(place_ref[0], stream_ref, facing_ref, outer_ref)
    mean = jnp.sum(acc, axis=0, keepdims=True) * (1.0 / ROWS)
    put_stats(stats_ref, mean, deviations((stream_ref,), mean, CH))


def pool_kernel(
    got_ref, gain_ref, bias_ref, point_ref, conv_ref, pool_ref, out_ref, gated_ref, sums_ref, flip_ref
):
    terms = norm_terms(1, got_ref, gain_ref, bias_ref)
    bins = TILE // POOL
    row = lax.broadcasted_iota(jnp.int32, (bins, TILE), 0)
    col = lax.broadcasted_iota(jnp.int32, (bins, TILE), 1)
    pick = jnp.where(col // POOL == row, 1.0, 0.0).astype(BF16)

    def tile(i, carry):
        gated = gated_tile(conv_ref, i, terms, gated_ref)
        sums_ref[row_slice(i, bins), :] = jnp.dot(pick, gated, preferred_element_type=F32)
        return carry

    lax.fori_loop(0, ROWS // TILE, tile, 0)
    sums = sums_ref[...]
    upper = sums.astype(BF16)
    lower = (sums - upper.astype(F32)).astype(BF16)
    branch = jnp.dot(upper, point_ref[1], preferred_element_type=F32)
    branch += jnp.dot(lower, point_ref[1], preferred_element_type=F32)
    flipped = ((pool_ref[...] + branch) * (1.0 / POOL)).T
    size = CH // HEADS
    for k in range(ROWS // POOL // 128):
        half = flip_ref.at[k]
        for h in range(HEADS):
            half[pl.ds(h, size, stride=HEADS), :] = flipped[h * size : (h + 1) * size, 128 * k : 128 * (k + 1)]
        out_ref[:, 128 * k : 128 * (k + 1)] = half[...]


VMEM = pl.BlockSpec(memory_space=pltpu.VMEM)
SMEM = pl.BlockSpec(memory_space=pltpu.SMEM)
PARAMS = pltpu.CompilerParams(vmem_limit_bytes=20 * 1024 * 1024)


def call(body, args, outs, scratch=(), scalars=0):
    return pl.pallas_call(
        body,
        out_shape=[jax.ShapeDtypeStruct(s, d) for s, d in outs],
        in_specs=[SMEM] * scalars + [VMEM] * (len(args) - scalars),
        out_specs=[VMEM] * len(outs),
        scratch_shapes=[pltpu.VMEM(s, d) for s, d in scratch],
        compiler_params=PARAMS,
    )(*args)


def reduce_stats(sent, first, second):
    got = lax.all_to_all(sent, first, 0, 0, tiled=True)
    rows = got.shape[1] // 2
    means = got[:, :rows]
    mean = jnp.mean(means, axis=0)
    spread = means - mean
    squares = jnp.sum(got[:, rows:], axis=0) + ROWS * jnp.sum(spread * spread, axis=0)
    both = jnp.concatenate([mean, squares])
    return lax.all_to_all(jnp.broadcast_to(both[None], sent.shape), second, 0, 0, tiled=True)


def halos(facing, outer):
    peers = lax.axis_size(SEQ)
    near = lax.ppermute(facing, SEQ, [(i, i ^ 1) for i in range(peers)])
    pairs = [(i, i + 1) for i in range(1, peers - 1, 2)]
    return near, lax.ppermute(outer, SEQ, pairs + [(j, i) for i, j in pairs])


def per_device(inputs, taps, point, in_gain, in_bias, mid_gain, mid_bias):
    place = lax.axis_index(SEQ)
    core = lax.axis_index("core")
    joined = jnp.where(core == 0, place > 0, place < lax.axis_size(SEQ) - 1)
    where = jnp.stack([core, joined.astype(core.dtype)]).astype(jnp.int32)
    x = inputs.reshape(ROWS, CH)
    wide_stats = ((PEERS, 8, 128), F32)
    slim_stats = ((PEERS, 4, 128), F32)
    conv_outs = [((ROWS, MID), F32), slim_stats]

    edge = ((NEAR, CH), BF16)
    facing, outer, stats = call(input_stats, (where, x), [edge, edge, wide_stats], scalars=1)
    near, cross = halos(facing, outer)
    got = reduce_stats(stats, ACROSS, ALONG)
    conv, stats = call(
        functools.partial(conv_kernel, 0, NEAR),
        (where, got, in_gain, in_bias, taps, near, x, cross),
        conv_outs,
        [((ROWS + 2 * NEAR, CH), BF16)],
        1,
    )
    got = reduce_stats(stats, ACROSS, ALONG)
    edge = ((FAR, CH), F32)
    stream, facing, outer, stats, pooled = call(
        point_kernel,
        (where, got, mid_gain, mid_bias, point, conv, x),
        [((ROWS, CH), F32), edge, edge, wide_stats, ((ROWS // POOL, CH), F32)],
        [((TILE, MID), BF16)],
        1,
    )
    near, cross = halos(facing, outer)
    got = reduce_stats(stats, ALONG, ACROSS)
    conv, stats = call(
        functools.partial(conv_kernel, 1, FAR),
        (where, got, in_gain, in_bias, taps, near, stream, cross),
        conv_outs,
        [((ROWS + 2 * FAR, CH), BF16)],
        1,
    )
    got = reduce_stats(stats, ACROSS, ALONG)
    (out,) = call(
        pool_kernel,
        (got, mid_gain, mid_bias, point, conv, pooled),
        [((CH, ROWS // POOL), F32)],
        [((TILE, MID), BF16), ((ROWS // POOL, MID), F32), ((ROWS // POOL // 128, CH, 128), F32)],
    )
    bins = ROWS // POOL
    out = lax.all_to_all(out.reshape(CH // HEADS, HEADS, bins), SEQ, 0, 0, tiled=True)
    peers = lax.axis_size(SEQ)
    out = out.reshape(peers, -1, HEADS, bins).transpose(2, 1, 0, 3)
    return out.reshape(1, HEADS, -1, peers * bins)


def solution(mesh):
    fine = Mesh(mesh.devices.reshape(SIZES), NAMES)
    return jax.shard_map(
        per_device,
        mesh=fine,
        in_specs=(P(BATCH, SEQ, None), P(), P(), P(), P(), P(), P()),
        out_specs=P(BATCH, None, SEQ, None),
        check_vma=False,
    )
```

```python
import functools

import jax
import jax.numpy as jnp
from jax import lax
from jax.experimental import pallas as pl
from jax.experimental.pallas import tpu as pltpu
from jax.sharding import Mesh, PartitionSpec as P

EPS = 1e-05
HEADS = 8
POOL = 8
ROWS = 2048
CH = 512
MID = 256
TILE = 256
CHUNK = 32
NEAR = 256
FAR = 512

NAMES = ("y_lo", "x", "z", "y_hi", "core")
SIZES = (2, 4, 8, 2, 2)
BATCH = ("y_lo", "x")
SEQ = ("z", "y_hi", "core")
ACROSS = ("y_lo", "x", "y_hi")
ALONG = ("z", "core")
PEERS = 16
COUNT = PEERS * PEERS * ROWS
TOP = 60000.0
F32 = jnp.float32
BF16 = jnp.bfloat16


def gelu(u):
    return 0.5 * u * (1.0 + lax.erf(u * 0.7071067811865476))


def wide(v):
    return jnp.concatenate([v[j : j + 1] for j in range(v.shape[0])], axis=1)


def combined(got_ref):
    rows = got_ref.shape[1] // 2
    got = got_ref[...]
    means = got[:, :rows]
    mean = jnp.sum(means, axis=0) * (1.0 / PEERS)
    spread = means - mean
    total = jnp.sum(got[:, rows:], axis=0) + (PEERS * ROWS) * jnp.sum(spread * spread, axis=0)
    return mean, total * (1.0 / COUNT)


def norm_terms(layer, got_ref, gain_ref, bias_ref):
    mean, variance = combined(got_ref)
    factor = gain_ref[layer : layer + 1] * lax.rsqrt(wide(variance) + EPS)
    return wide(mean), factor, bias_ref[layer : layer + 1]


def largest(v):
    return jnp.max(jnp.max(v, axis=0, keepdims=True), axis=1, keepdims=True)


def output_bound(stream_got_ref, gain_ref, bias_ref, point_ref):
    mean, variance = combined(stream_got_ref)
    root = 1.01 * COUNT**0.5
    stream = root * jnp.sqrt(largest(variance + mean * mean))
    gated = root * largest(jnp.abs(gain_ref[1:2])) + 1.01 * largest(jnp.abs(bias_ref[1:2]))
    weights = jnp.sum(jnp.abs(point_ref[1].astype(F32)), axis=0, keepdims=True)
    return stream + gated * largest(weights) + 1e-30


def fold(v):
    return jnp.sum(v.reshape(-1, 8, v.shape[-1]), axis=0)


def put_stats(out_ref, mean, squares):
    rows = out_ref.shape[1] // 2
    for j in range(rows):
        for base, v in ((0, mean), (rows, squares)):
            piece = v[:, 128 * j : 128 * (j + 1)].reshape(1, 1, 128)
            out_ref[:, base + j : base + j + 1, :] = jnp.broadcast_to(piece, (PEERS, 1, 128))


def row_slice(i, size):
    return pl.ds(pl.multiple_of(i * size, size), size)


def deviations(refs, mean, channels):
    squares = jnp.zeros((8, channels), F32)
    for ref in refs:

        def step(i, acc, ref=ref):
            d = ref[row_slice(i, 64), :].astype(F32) - mean
            return acc + fold(d * d)

        squares = lax.fori_loop(0, ref.shape[0] // 64, step, squares, unroll=4)
    return jnp.sum(squares, axis=0, keepdims=True)


def input_stats(place_ref, x_hbm, facing_ref, outer_ref, out_ref, x_ref, sems):
    parts = sems.shape[0]
    size = ROWS // parts
    copies = []
    for p in range(parts):
        rows = pl.ds(p * size, size)
        copies.append(pltpu.make_async_copy(x_hbm.at[rows], x_ref.at[rows], sems.at[p]))
        copies[p].start()
    means, squares = [], jnp.zeros((1, CH), F32)
    for p in range(parts):
        copies[p].wait()
        part = x_ref.at[p * size : (p + 1) * size]

        def step(i, acc, part=part):
            return acc + fold(part[row_slice(i, 64), :].astype(F32))

        acc = lax.fori_loop(0, size // 64, step, jnp.zeros((8, CH), F32), unroll=4)
        means.append(jnp.sum(acc, axis=0, keepdims=True) * (1.0 / size))
        squares += deviations((part,), means[p], CH)
    put_edges(place_ref[0], x_ref, facing_ref, outer_ref)
    mean = sum(means) * (1.0 / parts)
    put_stats(out_ref, mean, squares + size * sum((m - mean) * (m - mean) for m in means))


def activate(piece, first, count, terms, act_ref, offset, flag=None):
    mean, factor, bias = terms

    def step(i, carry):
        v = piece[pl.ds(pl.multiple_of(first + i * CHUNK, CHUNK), CHUNK), :].astype(F32)
        a = gelu((v - mean) * factor + bias)
        if flag is not None:
            a = jnp.where(flag > 0, a, 0.0)
        act_ref[pl.ds(pl.multiple_of(offset + i * CHUNK, CHUNK), CHUNK), :] = a.astype(BF16)
        return carry

    lax.fori_loop(0, count // CHUNK, step, 0)


def conv_stats(acc, center, stats_ref):
    mean = jnp.sum(acc, axis=0, keepdims=True) * (1.0 / ROWS)
    put_stats(stats_ref, mean, deviations((center,), mean, MID))


def conv_kernel(
    layer,
    dilation,
    size,
    place_ref,
    got_ref,
    gain_ref,
    bias_ref,
    taps_hbm,
    near_ref,
    center_ref,
    cross_ref,
    conv_ref,
    stats_ref,
    act_ref,
    taps_ref,
    taps_sem,
):
    copy = pltpu.make_async_copy(taps_hbm.at[layer], taps_ref, taps_sem)
    copy.start()
    terms = norm_terms(layer, got_ref, gain_ref, bias_ref)
    core = place_ref[0]
    activate(near_ref, 0, dilation, terms, act_ref, (1 - core) * (dilation + ROWS))
    activate(cross_ref, 0, dilation, terms, act_ref, core * (dilation + ROWS), place_ref[1])
    copy.wait()
    weights = taps_ref[...].reshape(3 * CH, MID)
    mean, factor, bias = terms
    acc = jnp.zeros((8, MID), F32)
    done = 0
    for end in range(size, ROWS + size, size):
        for r in range(end - size, end, CHUNK):
            v = center_ref[r : r + CHUNK, :].astype(F32)
            act_ref[dilation + r : dilation + r + CHUNK, :] = gelu((v - mean) * factor + bias).astype(BF16)
        ready = ROWS if end == ROWS else end - dilation
        while done + size <= ready:
            rows = [act_ref[done + k * dilation : done + k * dilation + size, :] for k in range(3)]
            total = jnp.dot(jnp.concatenate(rows, axis=1), weights, preferred_element_type=F32)
            conv_ref[done : done + size, :] = total
            acc = acc + fold(total)
            done += size
    conv_stats(acc, conv_ref, stats_ref)


def put_edges(core, rows_ref, facing_ref, outer_ref):
    size = facing_ref.shape[0]
    last = ROWS - size
    facing_ref[...] = rows_ref[pl.ds(pl.multiple_of((1 - core) * last, 256), size), :]
    outer_ref[...] = rows_ref[pl.ds(pl.multiple_of(core * last, 256), size), :]


def gated_tile(conv_ref, i, terms, gated_ref):
    mean, factor, bias = terms
    for r in range(i * TILE, (i + 1) * TILE, CHUNK):
        gated_ref[r : r + CHUNK, :] = gelu((conv_ref[r : r + CHUNK, :] - mean) * factor + bias).astype(BF16)
    return gated_ref[i * TILE : (i + 1) * TILE, :]


def point_kernel(
    place_ref,
    got_ref,
    gain_ref,
    bias_ref,
    point_ref,
    conv_ref,
    x_ref,
    stream_ref,
    facing_ref,
    outer_ref,
    stats_ref,
    pool_ref,
    gated_ref,
):
    terms = norm_terms(0, got_ref, gain_ref, bias_ref)
    acc = jnp.zeros((8, CH), F32)
    bins = TILE // POOL
    for i in range(ROWS // TILE):
        rows = slice(i * TILE, (i + 1) * TILE)
        gated = gated_tile(conv_ref, i, terms, gated_ref)
        total = x_ref[rows, :].astype(F32) + jnp.dot(gated, point_ref[0], preferred_element_type=F32)
        stream_ref[rows, :] = total
        pool_ref[i * bins : (i + 1) * bins, :] = jnp.sum(total.reshape(bins, POOL, CH), axis=1)
        acc = acc + fold(total)
    put_edges(place_ref[0], stream_ref, facing_ref, outer_ref)
    mean = jnp.sum(acc, axis=0, keepdims=True) * (1.0 / ROWS)
    put_stats(stats_ref, mean, deviations((stream_ref,), mean, CH))


def pool_kernel(
    got_ref,
    stream_got_ref,
    gain_ref,
    bias_ref,
    point_ref,
    conv_ref,
    pool_ref,
    out_ref,
    bound_ref,
    gated_ref,
    sums_ref,
    flip_ref,
):
    bound = output_bound(stream_got_ref, gain_ref, bias_ref, point_ref)
    bound_ref[...] = jnp.broadcast_to(bound * (1.0 / TOP), bound_ref.shape)
    scale = (TOP / POOL) / bound
    terms = norm_terms(1, got_ref, gain_ref, bias_ref)
    bins = TILE // POOL
    row = lax.broadcasted_iota(jnp.int32, (bins, TILE), 0)
    col = lax.broadcasted_iota(jnp.int32, (bins, TILE), 1)
    pick = jnp.where(col // POOL == row, 1.0, 0.0).astype(BF16)

    for i in range(ROWS // TILE):
        gated = gated_tile(conv_ref, i, terms, gated_ref)
        sums_ref[i * bins : (i + 1) * bins, :] = jnp.dot(pick, gated, preferred_element_type=F32)
    sums = sums_ref[...]
    upper = sums.astype(BF16)
    lower = (sums - upper.astype(F32)).astype(BF16)
    branch = jnp.dot(upper, point_ref[1], preferred_element_type=F32)
    branch += jnp.dot(lower, point_ref[1], preferred_element_type=F32)
    flipped = ((pool_ref[...] + branch) * scale).T
    size = CH // HEADS
    for k in range(ROWS // POOL // 128):
        half = flip_ref.at[k]
        for h in range(HEADS):
            half[pl.ds(h, size, stride=HEADS), :] = flipped[h * size : (h + 1) * size, 128 * k : 128 * (k + 1)]
        out_ref[:, 128 * k : 128 * (k + 1)] = half[...]


VMEM = pl.BlockSpec(memory_space=pltpu.VMEM)
SMEM = pl.BlockSpec(memory_space=pltpu.SMEM)
HBM = pl.BlockSpec(memory_space=pltpu.HBM)
PARAMS = pltpu.CompilerParams(vmem_limit_bytes=20 * 1024 * 1024)


def call(body, args, outs, scratch=(), scalars=0, far=()):
    specs = [SMEM if i < scalars else HBM if i in far else VMEM for i in range(len(args))]
    return pl.pallas_call(
        body,
        out_shape=[jax.ShapeDtypeStruct(s, d) for s, d in outs],
        in_specs=specs,
        out_specs=[VMEM] * len(outs),
        scratch_shapes=list(scratch),
        compiler_params=PARAMS,
    )(*args)


def reduce_stats(sent, first, second):
    got = lax.all_to_all(sent, first, 0, 0, tiled=True)
    rows = got.shape[1] // 2
    means = got[:, :rows]
    mean = jnp.mean(means, axis=0)
    spread = means - mean
    squares = jnp.sum(got[:, rows:], axis=0) + ROWS * jnp.sum(spread * spread, axis=0)
    both = jnp.concatenate([mean, squares])
    return lax.all_to_all(jnp.broadcast_to(both[None], sent.shape), second, 0, 0, tiled=True)


def halos(facing, outer):
    peers = lax.axis_size(SEQ)
    near = lax.ppermute(facing, SEQ, [(i, i ^ 1) for i in range(peers)])
    pairs = [(i, i + 1) for i in range(1, peers - 1, 2)]
    return near, lax.ppermute(outer, SEQ, pairs + [(j, i) for i, j in pairs])


def per_device(inputs, taps, point, in_gain, in_bias, mid_gain, mid_bias):
    place = lax.axis_index(SEQ)
    core = lax.axis_index("core")
    joined = jnp.where(core == 0, place > 0, place < lax.axis_size(SEQ) - 1)
    where = jnp.stack([core, joined.astype(core.dtype)]).astype(jnp.int32)
    x = inputs.reshape(ROWS, CH)
    wide_stats = ((PEERS, 8, 128), F32)
    slim_stats = ((PEERS, 4, 128), F32)
    conv_outs = [((ROWS, MID), F32), slim_stats]

    edge = ((NEAR, CH), BF16)
    facing, outer, stats = call(
        input_stats,
        (where, x),
        [edge, edge, wide_stats],
        [pltpu.VMEM((ROWS, CH), BF16), pltpu.SemaphoreType.DMA((4,))],
        1,
        (1,),
    )
    near, cross = halos(facing, outer)
    got = reduce_stats(stats, ACROSS, ALONG)
    conv, stats = call(
        functools.partial(conv_kernel, 0, NEAR, 256),
        (where, got, in_gain, in_bias, taps, near, x, cross),
        conv_outs,
        [pltpu.VMEM((ROWS + 2 * NEAR, CH), BF16), pltpu.VMEM((3, CH, MID), BF16), pltpu.SemaphoreType.DMA],
        1,
        (4,),
    )
    got = reduce_stats(stats, ACROSS, ALONG)
    edge = ((FAR, CH), F32)
    stream, facing, outer, stats, pooled = call(
        point_kernel,
        (where, got, mid_gain, mid_bias, point, conv, x),
        [((ROWS, CH), F32), edge, edge, wide_stats, ((ROWS // POOL, CH), F32)],
        [pltpu.VMEM((ROWS, MID), BF16)],
        1,
    )
    near, cross = halos(facing, outer)
    stream_got = reduce_stats(stats, ALONG, ACROSS)
    conv, stats = call(
        functools.partial(conv_kernel, 1, FAR, 512),
        (where, stream_got, in_gain, in_bias, taps, near, stream, cross),
        conv_outs,
        [pltpu.VMEM((ROWS + 2 * FAR, CH), BF16), pltpu.VMEM((3, CH, MID), BF16), pltpu.SemaphoreType.DMA],
        1,
        (4,),
    )
    got = reduce_stats(stats, ACROSS, ALONG)
    out, bound = call(
        pool_kernel,
        (got, stream_got, mid_gain, mid_bias, point, conv, pooled),
        [((CH, ROWS // POOL), F32), ((1, ROWS // POOL), F32)],
        [
            pltpu.VMEM((ROWS, MID), BF16),
            pltpu.VMEM((ROWS // POOL, MID), F32),
            pltpu.VMEM((ROWS // POOL // 128, CH, 128), F32),
        ],
    )
    bins = ROWS // POOL
    out = lax.all_to_all(out.reshape(CH // HEADS, HEADS, bins).astype(jnp.float16), SEQ, 0, 0, tiled=True)
    peers = lax.axis_size(SEQ)
    out = out.astype(F32).reshape(peers, -1, HEADS, bins) * bound.reshape(1, 1, 1, bins)
    return out.transpose(2, 1, 0, 3).reshape(1, HEADS, -1, peers * bins)


def solution(mesh):
    fine = Mesh(mesh.devices.reshape(SIZES), NAMES)
    return jax.shard_map(
        per_device,
        mesh=fine,
        in_specs=(P(BATCH, SEQ, None), P(), P(), P(), P(), P(), P()),
        out_specs=P(BATCH, None, SEQ, None),
        check_vma=False,
    )
```

```python
import jax
import jax.numpy as jnp
from jax import lax
from jax.experimental import pallas as pl
from jax.experimental.pallas import tpu as pltpu
from jax.sharding import Mesh, PartitionSpec as P

EPS = 1e-05
HEADS = 8
POOL = 8
ROWS = 2048
CH = 512
MID = 256
TILE = 256
CHUNK = 32
NEAR = 256
FAR = 512

NAMES = ("y_lo", "x", "z", "y_hi", "core")
SIZES = (2, 4, 8, 2, 2)
BATCH = ("y_lo", "x")
SEQ = ("z", "y_hi", "core")
ACROSS = ("y_lo", "x", "y_hi")
ALONG = ("z", "core")
PEERS = 16
COUNT = PEERS * PEERS * ROWS
TOP = 60000.0
F32 = jnp.float32
BF16 = jnp.bfloat16


def gelu(u):
    return 0.5 * u * (1.0 + lax.erf(u * 0.7071067811865476))


def wide(v):
    return jnp.concatenate([v[j : j + 1] for j in range(v.shape[0])], axis=1)


def combined(got_ref):
    rows = got_ref.shape[1] // 2
    got = got_ref[...]
    means = got[:, :rows]
    mean = jnp.sum(means, axis=0) * (1.0 / PEERS)
    spread = means - mean
    total = jnp.sum(got[:, rows:], axis=0) + (PEERS * ROWS) * jnp.sum(spread * spread, axis=0)
    return mean, total * (1.0 / COUNT)


def norm_terms(layer, got_ref, gain_ref, bias_ref):
    mean, variance = combined(got_ref)
    factor = gain_ref[layer : layer + 1] * lax.rsqrt(wide(variance) + EPS)
    return wide(mean), factor, bias_ref[layer : layer + 1]


def largest(v):
    return jnp.max(jnp.max(v, axis=0, keepdims=True), axis=1, keepdims=True)


def output_bound(stream_got_ref, gain_ref, bias_ref, point_ref):
    mean, variance = combined(stream_got_ref)
    root = 1.01 * COUNT**0.5
    stream = root * jnp.sqrt(largest(variance + mean * mean))
    gated = root * largest(jnp.abs(gain_ref[1:2])) + 1.01 * largest(jnp.abs(bias_ref[1:2]))
    weights = jnp.sum(jnp.abs(point_ref[1].astype(F32)), axis=0, keepdims=True)
    return stream + gated * largest(weights) + 1e-30


def fold(v):
    return jnp.sum(v.reshape(-1, 8, v.shape[-1]), axis=0)


def put_stats(out_ref, mean, squares):
    rows = out_ref.shape[1] // 2
    for j in range(rows):
        for base, v in ((0, mean), (rows, squares)):
            piece = v[:, 128 * j : 128 * (j + 1)].reshape(1, 1, 128)
            out_ref[:, base + j : base + j + 1, :] = jnp.broadcast_to(piece, (PEERS, 1, 128))


def row_slice(i, size):
    return pl.ds(pl.multiple_of(i * size, size), size)


def deviations(refs, mean, channels):
    squares = jnp.zeros((8, channels), F32)
    for ref in refs:

        def step(i, acc, ref=ref):
            d = ref[row_slice(i, 64), :].astype(F32) - mean
            return acc + fold(d * d)

        squares = lax.fori_loop(0, ref.shape[0] // 64, step, squares, unroll=4)
    return jnp.sum(squares, axis=0, keepdims=True)


def input_stats(place_ref, x_ref, facing_ref, outer_ref, out_ref):
    put_edges(place_ref[0], x_ref, facing_ref, outer_ref)
    acc = jnp.zeros((8, CH), F32)
    for r in range(0, ROWS, 64):
        acc += fold(x_ref[r : r + 64, :].astype(F32))
    mean = jnp.sum(acc, axis=0, keepdims=True) * (1.0 / ROWS)
    squares = jnp.zeros((8, CH), F32)
    for r in range(0, ROWS, 64):
        d = x_ref[r : r + 64, :].astype(F32) - mean
        squares += fold(d * d)
    put_stats(out_ref, mean, jnp.sum(squares, axis=0, keepdims=True))


def activate(piece, first, count, terms, act_ref, offset, flag=None):
    mean, factor, bias = terms

    def step(i, carry):
        v = piece[pl.ds(pl.multiple_of(first + i * CHUNK, CHUNK), CHUNK), :].astype(F32)
        a = gelu((v - mean) * factor + bias)
        if flag is not None:
            a = jnp.where(flag > 0, a, 0.0)
        act_ref[pl.ds(pl.multiple_of(offset + i * CHUNK, CHUNK), CHUNK), :] = a.astype(BF16)
        return carry

    lax.fori_loop(0, count // CHUNK, step, 0)


def conv_stats(acc, center, stats_ref):
    mean = jnp.sum(acc, axis=0, keepdims=True) * (1.0 / ROWS)
    put_stats(stats_ref, mean, deviations((center,), mean, MID))


def conv_tiles(dilation, size, terms, center_ref, weights, conv_ref, stats_ref, act_ref):
    mean, factor, bias = terms
    acc = jnp.zeros((8, MID), F32)
    done = 0
    for end in range(size, ROWS + size, size):
        for r in range(end - size, end, CHUNK):
            v = center_ref[r : r + CHUNK, :].astype(F32)
            act_ref[dilation + r : dilation + r + CHUNK, :] = gelu((v - mean) * factor + bias).astype(BF16)
        ready = ROWS if end == ROWS else end - dilation
        while done + size <= ready:
            rows = [act_ref[done + k * dilation : done + k * dilation + size, :] for k in range(3)]
            total = jnp.dot(jnp.concatenate(rows, axis=1), weights, preferred_element_type=F32)
            conv_ref[done : done + size, :] = total
            acc = acc + fold(total)
            done += size
    conv_stats(acc, conv_ref, stats_ref)


def first_conv(
    place_ref,
    got_ref,
    gain_ref,
    bias_ref,
    taps_ref,
    near_ref,
    center_ref,
    cross_ref,
    conv_ref,
    stats_ref,
    act_ref,
):
    terms = norm_terms(0, got_ref, gain_ref, bias_ref)
    core = place_ref[0]
    activate(near_ref, core * (FAR - NEAR), NEAR, terms, act_ref, (1 - core) * (NEAR + ROWS))
    activate(cross_ref, (1 - core) * (FAR - NEAR), NEAR, terms, act_ref, core * (NEAR + ROWS), place_ref[1])
    weights = taps_ref[0].reshape(3 * CH, MID)
    conv_tiles(NEAR, 256, terms, center_ref, weights, conv_ref, stats_ref, act_ref)


def second_conv(
    place_ref,
    got_ref,
    gain_ref,
    bias_ref,
    taps_ref,
    point_ref,
    near_ref,
    near_gated_ref,
    center_ref,
    cross_ref,
    cross_gated_ref,
    conv_ref,
    stats_ref,
    act_ref,
    near_stream_ref,
    cross_stream_ref,
):
    terms = norm_terms(1, got_ref, gain_ref, bias_ref)
    core = place_ref[0]
    for x_ref, gated_ref, stream_ref in (
        (near_ref, near_gated_ref, near_stream_ref),
        (cross_ref, cross_gated_ref, cross_stream_ref),
    ):
        branch = jnp.dot(gated_ref[...], point_ref[0], preferred_element_type=F32)
        stream_ref[...] = x_ref[...].astype(F32) + branch
    activate(near_stream_ref, 0, FAR, terms, act_ref, (1 - core) * (FAR + ROWS))
    activate(cross_stream_ref, 0, FAR, terms, act_ref, core * (FAR + ROWS), place_ref[1])
    weights = taps_ref[1].reshape(3 * CH, MID)
    conv_tiles(FAR, 512, terms, center_ref, weights, conv_ref, stats_ref, act_ref)


def put_edges(core, rows_ref, facing_ref, outer_ref):
    size = facing_ref.shape[0]
    last = ROWS - size
    facing_ref[...] = rows_ref[pl.ds(pl.multiple_of((1 - core) * last, 256), size), :]
    outer_ref[...] = rows_ref[pl.ds(pl.multiple_of(core * last, 256), size), :]


def gated_tile(conv_ref, i, terms, gated_ref):
    mean, factor, bias = terms
    for r in range(i * TILE, (i + 1) * TILE, CHUNK):
        gated_ref[r : r + CHUNK, :] = gelu((conv_ref[r : r + CHUNK, :] - mean) * factor + bias).astype(BF16)
    return gated_ref[i * TILE : (i + 1) * TILE, :]


def point_kernel(
    place_ref,
    got_ref,
    gain_ref,
    bias_ref,
    point_ref,
    conv_ref,
    x_ref,
    stream_ref,
    facing_ref,
    outer_ref,
    stats_ref,
    pool_ref,
    gated_ref,
):
    terms = norm_terms(0, got_ref, gain_ref, bias_ref)
    acc = jnp.zeros((8, CH), F32)
    bins = TILE // POOL
    for i in range(ROWS // TILE):
        rows = slice(i * TILE, (i + 1) * TILE)
        gated = gated_tile(conv_ref, i, terms, gated_ref)
        total = x_ref[rows, :].astype(F32) + jnp.dot(gated, point_ref[0], preferred_element_type=F32)
        stream_ref[rows, :] = total
        pool_ref[i * bins : (i + 1) * bins, :] = jnp.sum(total.reshape(bins, POOL, CH), axis=1)
        acc = acc + fold(total)
    put_edges(place_ref[0], gated_ref, facing_ref, outer_ref)
    mean = jnp.sum(acc, axis=0, keepdims=True) * (1.0 / ROWS)
    put_stats(stats_ref, mean, deviations((stream_ref,), mean, CH))


def pool_kernel(
    got_ref,
    stream_got_ref,
    gain_ref,
    bias_ref,
    point_ref,
    conv_ref,
    pool_ref,
    out_ref,
    bound_ref,
    gated_ref,
    sums_ref,
    flip_ref,
):
    bound = output_bound(stream_got_ref, gain_ref, bias_ref, point_ref)
    bound_ref[...] = jnp.broadcast_to(bound * (1.0 / TOP), bound_ref.shape)
    scale = (TOP / POOL) / bound
    terms = norm_terms(1, got_ref, gain_ref, bias_ref)
    bins = TILE // POOL
    row = lax.broadcasted_iota(jnp.int32, (bins, TILE), 0)
    col = lax.broadcasted_iota(jnp.int32, (bins, TILE), 1)
    pick = jnp.where(col // POOL == row, 1.0, 0.0).astype(BF16)

    for i in range(ROWS // TILE):
        gated = gated_tile(conv_ref, i, terms, gated_ref)
        sums_ref[i * bins : (i + 1) * bins, :] = jnp.dot(pick, gated, preferred_element_type=F32)
    sums = sums_ref[...]
    upper = sums.astype(BF16)
    lower = (sums - upper.astype(F32)).astype(BF16)
    branch = jnp.dot(upper, point_ref[1], preferred_element_type=F32)
    branch += jnp.dot(lower, point_ref[1], preferred_element_type=F32)
    flipped = ((pool_ref[...] + branch) * scale).T
    size = CH // HEADS
    for k in range(ROWS // POOL // 128):
        half = flip_ref.at[k]
        for h in range(HEADS):
            half[pl.ds(h, size, stride=HEADS), :] = flipped[h * size : (h + 1) * size, 128 * k : 128 * (k + 1)]
        out_ref[:, 128 * k : 128 * (k + 1)] = half[...]


VMEM = pl.BlockSpec(memory_space=pltpu.VMEM)
SMEM = pl.BlockSpec(memory_space=pltpu.SMEM)
PARAMS = pltpu.CompilerParams(vmem_limit_bytes=20 * 1024 * 1024)


def call(body, args, outs, scratch=(), scalars=0):
    return pl.pallas_call(
        body,
        out_shape=[jax.ShapeDtypeStruct(s, d) for s, d in outs],
        in_specs=[SMEM] * scalars + [VMEM] * (len(args) - scalars),
        out_specs=[VMEM] * len(outs),
        scratch_shapes=list(scratch),
        compiler_params=PARAMS,
    )(*args)


def halos(facing, outer):
    peers = lax.axis_size(SEQ)
    near = lax.ppermute(facing, SEQ, [(i, i ^ 1) for i in range(peers)])
    pairs = [(i, i + 1) for i in range(1, peers - 1, 2)]
    return near, lax.ppermute(outer, SEQ, pairs + [(j, i) for i, j in pairs])


def reduce_stats(sent, first, second, *edges):
    got = lax.all_to_all(sent, first, 0, 0, tiled=True)
    rows = got.shape[1] // 2
    means = got[:, :rows]
    mean = jnp.mean(means, axis=0)
    spread = means - mean
    squares = jnp.sum(got[:, rows:], axis=0) + ROWS * jnp.sum(spread * spread, axis=0)
    both = jnp.concatenate([mean, squares])
    if edges:
        both, *edges = lax.optimization_barrier((both, *edges))
        edges = halos(*edges)
    return lax.all_to_all(jnp.broadcast_to(both[None], sent.shape), second, 0, 0, tiled=True), *edges


def per_device(inputs, taps, point, in_gain, in_bias, mid_gain, mid_bias):
    place = lax.axis_index(SEQ)
    core = lax.axis_index("core")
    joined = jnp.where(core == 0, place > 0, place < lax.axis_size(SEQ) - 1)
    where = jnp.stack([core, joined.astype(core.dtype)]).astype(jnp.int32)
    x = inputs.reshape(ROWS, CH)
    wide_stats = ((PEERS, 8, 128), F32)
    slim_stats = ((PEERS, 4, 128), F32)
    conv_outs = [((ROWS, MID), F32), slim_stats]

    edge = ((FAR, CH), BF16)
    facing, outer, stats = call(
        input_stats,
        (where, x),
        [edge, edge, wide_stats],
        scalars=1,
    )
    got, near, cross = reduce_stats(stats, ACROSS, ALONG, facing, outer)
    conv, stats = call(
        first_conv,
        (where, got, in_gain, in_bias, taps, near, x, cross),
        conv_outs,
        [pltpu.VMEM((ROWS + 2 * NEAR, CH), BF16)],
        1,
    )
    (got,) = reduce_stats(stats, ACROSS, ALONG)
    edge = ((FAR, MID), BF16)
    stream, facing, outer, stats, pooled = call(
        point_kernel,
        (where, got, mid_gain, mid_bias, point, conv, x),
        [((ROWS, CH), F32), edge, edge, wide_stats, ((ROWS // POOL, CH), F32)],
        [pltpu.VMEM((ROWS, MID), BF16)],
        1,
    )
    stream_got, near_gated, cross_gated = reduce_stats(stats, ACROSS, ALONG, facing, outer)
    conv, stats = call(
        second_conv,
        (where, stream_got, in_gain, in_bias, taps, point, near, near_gated, stream, cross, cross_gated),
        conv_outs,
        [
            pltpu.VMEM((ROWS + 2 * FAR, CH), BF16),
            pltpu.VMEM((FAR, CH), F32),
            pltpu.VMEM((FAR, CH), F32),
        ],
        1,
    )
    (got,) = reduce_stats(stats, ACROSS, ALONG)
    out, bound = call(
        pool_kernel,
        (got, stream_got, mid_gain, mid_bias, point, conv, pooled),
        [((CH, ROWS // POOL), F32), ((1, ROWS // POOL), F32)],
        [
            pltpu.VMEM((ROWS, MID), BF16),
            pltpu.VMEM((ROWS // POOL, MID), F32),
            pltpu.VMEM((ROWS // POOL // 128, CH, 128), F32),
        ],
    )
    bins = ROWS // POOL
    out = lax.all_to_all(out.reshape(CH // HEADS, HEADS, bins).astype(jnp.float16), SEQ, 0, 0, tiled=True)
    peers = lax.axis_size(SEQ)
    out = out.astype(F32).reshape(peers, -1, HEADS, bins) * bound.reshape(1, 1, 1, bins)
    return out.transpose(2, 1, 0, 3).reshape(1, HEADS, -1, peers * bins)


def solution(mesh):
    fine = Mesh(mesh.devices.reshape(SIZES), NAMES)
    return jax.shard_map(
        per_device,
        mesh=fine,
        in_specs=(P(BATCH, SEQ, None), P(), P(), P(), P(), P(), P()),
        out_specs=P(BATCH, None, SEQ, None),
        check_vma=False,
    )
```

```python
import jax
import jax.numpy as jnp
from jax import lax
from jax.experimental import pallas as pl
from jax.experimental.pallas import tpu as pltpu
from jax.sharding import Mesh, PartitionSpec as P

EPS = 1e-05
HEADS = 8
POOL = 8
ROWS = 2048
CH = 512
MID = 256
TILE = 256
CHUNK = 32
NEAR = 256
FAR = 512

NAMES = ("y_lo", "x", "z", "y_hi", "core")
SIZES = (2, 4, 8, 2, 2)
BATCH = ("y_lo", "x")
SEQ = ("z", "y_hi", "core")
ACROSS = ("y_lo", "x", "y_hi")
ALONG = ("z", "core")
PEERS = 16
COUNT = PEERS * PEERS * ROWS
TOP = 60000.0
F32 = jnp.float32
BF16 = jnp.bfloat16


def gelu(u):
    return 0.5 * u * (1.0 + lax.erf(u * 0.7071067811865476))


def wide(v):
    return jnp.concatenate([v[j : j + 1] for j in range(v.shape[0])], axis=1)


def combined(got_ref):
    rows = got_ref.shape[1] // 2
    got = got_ref[...]
    means = got[:, :rows]
    mean = jnp.sum(means, axis=0) * (1.0 / PEERS)
    spread = means - mean
    total = jnp.sum(got[:, rows:], axis=0) + (PEERS * ROWS) * jnp.sum(spread * spread, axis=0)
    return mean, total * (1.0 / COUNT)


def norm_terms(layer, got_ref, gain_ref, bias_ref):
    mean, variance = combined(got_ref)
    factor = gain_ref[layer : layer + 1] * lax.rsqrt(wide(variance) + EPS)
    return wide(mean), factor, bias_ref[layer : layer + 1]


def largest(v):
    return jnp.max(jnp.max(v, axis=0, keepdims=True), axis=1, keepdims=True)


def output_bound(stream_got_ref, gain_ref, bias_ref, point_ref):
    mean, variance = combined(stream_got_ref)
    root = 1.01 * COUNT**0.5
    stream = root * jnp.sqrt(largest(variance + mean * mean))
    gated = root * largest(jnp.abs(gain_ref[1:2])) + 1.01 * largest(jnp.abs(bias_ref[1:2]))
    weights = jnp.sum(jnp.abs(point_ref[1].astype(F32)), axis=0, keepdims=True)
    return stream + gated * largest(weights) + 1e-30


def fold(v):
    return jnp.sum(v.reshape(-1, 8, v.shape[-1]), axis=0)


def put_stats(out_ref, mean, squares):
    rows = out_ref.shape[1] // 2
    for j in range(rows):
        for base, v in ((0, mean), (rows, squares)):
            piece = v[:, 128 * j : 128 * (j + 1)].reshape(1, 1, 128)
            out_ref[:, base + j : base + j + 1, :] = jnp.broadcast_to(piece, (PEERS, 1, 128))


def row_slice(i, size):
    return pl.ds(pl.multiple_of(i * size, size), size)


def deviations(refs, mean, channels):
    squares = jnp.zeros((8, channels), F32)
    for ref in refs:

        def step(i, acc, ref=ref):
            d = ref[row_slice(i, 64), :].astype(F32) - mean
            return acc + fold(d * d)

        squares = lax.fori_loop(0, ref.shape[0] // 64, step, squares, unroll=4)
    return jnp.sum(squares, axis=0, keepdims=True)


def pack_edges(core, gated_ref, x_ref, facing_ref, outer_ref):
    put_edges(core, gated_ref, facing_ref.at[:, :MID], outer_ref.at[:, :MID])
    for last, edge_ref in ((1 - core, facing_ref), (core, outer_ref)):
        rows = pl.ds(pl.multiple_of(NEAR + last * (ROWS - FAR - NEAR), NEAR), NEAR)
        edge_ref[:NEAR, MID:] = x_ref[rows, :MID]
        edge_ref[NEAR:, MID:] = x_ref[rows, MID:]


def input_stats(place_ref, x_ref, facing_ref, outer_ref, out_ref):
    put_edges(place_ref[0], x_ref, facing_ref, outer_ref)
    acc = jnp.zeros((8, CH), F32)
    for r in range(0, ROWS, 64):
        acc += fold(x_ref[r : r + 64, :].astype(F32))
    mean = jnp.sum(acc, axis=0, keepdims=True) * (1.0 / ROWS)
    squares = jnp.zeros((8, CH), F32)
    for r in range(0, ROWS, 64):
        d = x_ref[r : r + 64, :].astype(F32) - mean
        squares += fold(d * d)
    put_stats(out_ref, mean, jnp.sum(squares, axis=0, keepdims=True))


def activate(piece, first, count, terms, act_ref, offset, flag=None):
    mean, factor, bias = terms

    def step(i, carry):
        v = piece[pl.ds(pl.multiple_of(first + i * CHUNK, CHUNK), CHUNK), :].astype(F32)
        a = gelu((v - mean) * factor + bias)
        if flag is not None:
            a = jnp.where(flag > 0, a, 0.0)
        act_ref[pl.ds(pl.multiple_of(offset + i * CHUNK, CHUNK), CHUNK), :] = a.astype(BF16)
        return carry

    lax.fori_loop(0, count // CHUNK, step, 0)


def conv_stats(acc, center, stats_ref):
    mean = jnp.sum(acc, axis=0, keepdims=True) * (1.0 / ROWS)
    put_stats(stats_ref, mean, deviations((center,), mean, MID))


def conv_tiles(dilation, size, terms, center_ref, weights, conv_ref, stats_ref, act_ref):
    mean, factor, bias = terms
    acc = jnp.zeros((8, MID), F32)
    done = 0
    for end in range(size, ROWS + size, size):
        for r in range(end - size, end, CHUNK):
            v = center_ref[r : r + CHUNK, :].astype(F32)
            act_ref[dilation + r : dilation + r + CHUNK, :] = gelu((v - mean) * factor + bias).astype(BF16)
        ready = ROWS if end == ROWS else end - dilation
        while done + size <= ready:
            rows = [act_ref[done + k * dilation : done + k * dilation + size, :] for k in range(3)]
            total = jnp.dot(jnp.concatenate(rows, axis=1), weights, preferred_element_type=F32)
            conv_ref[done : done + size, :] = total
            acc = acc + fold(total)
            done += size
    conv_stats(acc, conv_ref, stats_ref)


def first_conv(
    place_ref,
    got_ref,
    gain_ref,
    bias_ref,
    taps_ref,
    near_ref,
    center_ref,
    cross_ref,
    conv_ref,
    stats_ref,
    act_ref,
):
    terms = norm_terms(0, got_ref, gain_ref, bias_ref)
    core = place_ref[0]
    activate(near_ref, 0, NEAR, terms, act_ref, (1 - core) * (NEAR + ROWS))
    activate(cross_ref, 0, NEAR, terms, act_ref, core * (NEAR + ROWS), place_ref[1])
    weights = taps_ref[0].reshape(3 * CH, MID)
    conv_tiles(NEAR, 256, terms, center_ref, weights, conv_ref, stats_ref, act_ref)


def second_conv(
    place_ref,
    got_ref,
    gain_ref,
    bias_ref,
    taps_ref,
    point_ref,
    near_ref,
    near_packed_ref,
    center_ref,
    cross_ref,
    cross_packed_ref,
    conv_ref,
    stats_ref,
    act_ref,
    near_stream_ref,
    cross_stream_ref,
):
    terms = norm_terms(1, got_ref, gain_ref, bias_ref)
    core = place_ref[0]
    for side, x_ref, packed_ref, stream_ref in (
        (core, near_ref, near_packed_ref, near_stream_ref),
        (1 - core, cross_ref, cross_packed_ref, cross_stream_ref),
    ):
        stream_ref[...] = jnp.dot(packed_ref[:, :MID], point_ref[0], preferred_element_type=F32)
        close = pl.ds(pl.multiple_of(side * NEAR, NEAR), NEAR)
        distant = pl.ds(pl.multiple_of((1 - side) * NEAR, NEAR), NEAR)
        stream_ref[close, :] += x_ref[...].astype(F32)
        stream_ref[distant, :MID] += packed_ref[:NEAR, MID:].astype(F32)
        stream_ref[distant, MID:] += packed_ref[NEAR:, MID:].astype(F32)
    activate(near_stream_ref, 0, FAR, terms, act_ref, (1 - core) * (FAR + ROWS))
    activate(cross_stream_ref, 0, FAR, terms, act_ref, core * (FAR + ROWS), place_ref[1])
    weights = taps_ref[1].reshape(3 * CH, MID)
    conv_tiles(FAR, 512, terms, center_ref, weights, conv_ref, stats_ref, act_ref)


def put_edges(core, rows_ref, facing_ref, outer_ref):
    size = facing_ref.shape[0]
    last = ROWS - size
    facing_ref[...] = rows_ref[pl.ds(pl.multiple_of((1 - core) * last, 256), size), :]
    outer_ref[...] = rows_ref[pl.ds(pl.multiple_of(core * last, 256), size), :]


def gated_tile(conv_ref, i, terms, gated_ref):
    mean, factor, bias = terms
    for r in range(i * TILE, (i + 1) * TILE, CHUNK):
        gated_ref[r : r + CHUNK, :] = gelu((conv_ref[r : r + CHUNK, :] - mean) * factor + bias).astype(BF16)
    return gated_ref[i * TILE : (i + 1) * TILE, :]


def point_kernel(
    place_ref,
    got_ref,
    gain_ref,
    bias_ref,
    point_ref,
    conv_ref,
    x_ref,
    stream_ref,
    facing_ref,
    outer_ref,
    stats_ref,
    pool_ref,
    gated_ref,
):
    terms = norm_terms(0, got_ref, gain_ref, bias_ref)
    acc = jnp.zeros((8, CH), F32)
    bins = TILE // POOL
    for i in range(ROWS // TILE):
        rows = slice(i * TILE, (i + 1) * TILE)
        gated = gated_tile(conv_ref, i, terms, gated_ref)
        total = x_ref[rows, :].astype(F32) + jnp.dot(gated, point_ref[0], preferred_element_type=F32)
        stream_ref[rows, :] = total
        pool_ref[i * bins : (i + 1) * bins, :] = jnp.sum(total.reshape(bins, POOL, CH), axis=1)
        acc = acc + fold(total)
    pack_edges(place_ref[0], gated_ref, x_ref, facing_ref, outer_ref)
    mean = jnp.sum(acc, axis=0, keepdims=True) * (1.0 / ROWS)
    put_stats(stats_ref, mean, deviations((stream_ref,), mean, CH))


def pool_kernel(
    got_ref,
    stream_got_ref,
    gain_ref,
    bias_ref,
    point_ref,
    conv_ref,
    pool_ref,
    out_ref,
    bound_ref,
    gated_ref,
    sums_ref,
    flip_ref,
):
    bound = output_bound(stream_got_ref, gain_ref, bias_ref, point_ref)
    bound_ref[...] = jnp.broadcast_to(bound * (1.0 / TOP), bound_ref.shape)
    scale = (TOP / POOL) / bound
    terms = norm_terms(1, got_ref, gain_ref, bias_ref)
    bins = TILE // POOL
    row = lax.broadcasted_iota(jnp.int32, (bins, TILE), 0)
    col = lax.broadcasted_iota(jnp.int32, (bins, TILE), 1)
    pick = jnp.where(col // POOL == row, 1.0, 0.0).astype(BF16)

    for i in range(ROWS // TILE):
        gated = gated_tile(conv_ref, i, terms, gated_ref)
        sums_ref[i * bins : (i + 1) * bins, :] = jnp.dot(pick, gated, preferred_element_type=F32)
    sums = sums_ref[...]
    upper = sums.astype(BF16)
    lower = (sums - upper.astype(F32)).astype(BF16)
    branch = jnp.dot(upper, point_ref[1], preferred_element_type=F32)
    branch += jnp.dot(lower, point_ref[1], preferred_element_type=F32)
    flipped = ((pool_ref[...] + branch) * scale).T
    size = CH // HEADS
    for k in range(ROWS // POOL // 128):
        half = flip_ref.at[k]
        for h in range(HEADS):
            half[pl.ds(h, size, stride=HEADS), :] = flipped[h * size : (h + 1) * size, 128 * k : 128 * (k + 1)]
        out_ref[:, 128 * k : 128 * (k + 1)] = half[...]


VMEM = pl.BlockSpec(memory_space=pltpu.VMEM)
SMEM = pl.BlockSpec(memory_space=pltpu.SMEM)
PARAMS = pltpu.CompilerParams(vmem_limit_bytes=20 * 1024 * 1024)


def call(body, args, outs, scratch=(), scalars=0):
    return pl.pallas_call(
        body,
        out_shape=[jax.ShapeDtypeStruct(s, d) for s, d in outs],
        in_specs=[SMEM] * scalars + [VMEM] * (len(args) - scalars),
        out_specs=[VMEM] * len(outs),
        scratch_shapes=list(scratch),
        compiler_params=PARAMS,
    )(*args)


def halos(facing, outer):
    peers = lax.axis_size(SEQ)
    near = lax.ppermute(facing, SEQ, [(i, i ^ 1) for i in range(peers)])
    pairs = [(i, i + 1) for i in range(1, peers - 1, 2)]
    return near, lax.ppermute(outer, SEQ, pairs + [(j, i) for i, j in pairs])


def reduce_stats(sent, first, second, *edges):
    got = lax.all_to_all(sent, first, 0, 0, tiled=True)
    rows = got.shape[1] // 2
    means = got[:, :rows]
    mean = jnp.mean(means, axis=0)
    spread = means - mean
    squares = jnp.sum(got[:, rows:], axis=0) + ROWS * jnp.sum(spread * spread, axis=0)
    both = jnp.concatenate([mean, squares])
    if edges:
        both, *edges = lax.optimization_barrier((both, *edges))
        edges = halos(*edges)
    return lax.all_to_all(jnp.broadcast_to(both[None], sent.shape), second, 0, 0, tiled=True), *edges


def per_device(inputs, taps, point, in_gain, in_bias, mid_gain, mid_bias):
    place = lax.axis_index(SEQ)
    core = lax.axis_index("core")
    joined = jnp.where(core == 0, place > 0, place < lax.axis_size(SEQ) - 1)
    where = jnp.stack([core, joined.astype(core.dtype)]).astype(jnp.int32)
    x = inputs.reshape(ROWS, CH)
    wide_stats = ((PEERS, 8, 128), F32)
    slim_stats = ((PEERS, 4, 128), F32)
    conv_outs = [((ROWS, MID), F32), slim_stats]

    edge = ((NEAR, CH), BF16)
    facing, outer, stats = call(
        input_stats,
        (where, x),
        [edge, edge, wide_stats],
        scalars=1,
    )
    near, cross = halos(facing, outer)
    (got,) = reduce_stats(stats, ACROSS, ALONG)
    conv, stats = call(
        first_conv,
        (where, got, in_gain, in_bias, taps, near, x, cross),
        conv_outs,
        [pltpu.VMEM((ROWS + 2 * NEAR, CH), BF16)],
        1,
    )
    (got,) = reduce_stats(stats, ACROSS, ALONG)
    edge = ((FAR, CH), BF16)
    stream, facing, outer, stats, pooled = call(
        point_kernel,
        (where, got, mid_gain, mid_bias, point, conv, x),
        [((ROWS, CH), F32), edge, edge, wide_stats, ((ROWS // POOL, CH), F32)],
        [pltpu.VMEM((ROWS, MID), BF16)],
        1,
    )
    stream_got, near_packed, cross_packed = reduce_stats(stats, ACROSS, ALONG, facing, outer)
    conv, stats = call(
        second_conv,
        (where, stream_got, in_gain, in_bias, taps, point, near, near_packed, stream, cross, cross_packed),
        conv_outs,
        [
            pltpu.VMEM((ROWS + 2 * FAR, CH), BF16),
            pltpu.VMEM((FAR, CH), F32),
            pltpu.VMEM((FAR, CH), F32),
        ],
        1,
    )
    (got,) = reduce_stats(stats, ACROSS, ALONG)
    out, bound = call(
        pool_kernel,
        (got, stream_got, mid_gain, mid_bias, point, conv, pooled),
        [((CH, ROWS // POOL), F32), ((1, ROWS // POOL), F32)],
        [
            pltpu.VMEM((ROWS, MID), BF16),
            pltpu.VMEM((ROWS // POOL, MID), F32),
            pltpu.VMEM((ROWS // POOL // 128, CH, 128), F32),
        ],
    )
    bins = ROWS // POOL
    out = lax.all_to_all(out.reshape(CH // HEADS, HEADS, bins).astype(jnp.float16), SEQ, 0, 0, tiled=True)
    peers = lax.axis_size(SEQ)
    out = out.astype(F32).reshape(peers, -1, HEADS, bins) * bound.reshape(1, 1, 1, bins)
    return out.transpose(2, 1, 0, 3).reshape(1, HEADS, -1, peers * bins)


def solution(mesh):
    fine = Mesh(mesh.devices.reshape(SIZES), NAMES)
    return jax.shard_map(
        per_device,
        mesh=fine,
        in_specs=(P(BATCH, SEQ, None), P(), P(), P(), P(), P(), P()),
        out_specs=P(BATCH, None, SEQ, None),
        check_vma=False,
    )
```

```python
import jax
import jax.numpy as jnp
from jax import lax
from jax.experimental import pallas as pl
from jax.experimental.pallas import tpu as pltpu
from jax.sharding import Mesh, PartitionSpec as P

EPS = 1e-05
HEADS = 8
POOL = 8
ROWS = 2048
CH = 512
MID = 256
TILE = 256
CHUNK = 32
NEAR = 256
FAR = 512

NAMES = ("y_lo", "x", "z", "y_hi", "core")
SIZES = (2, 4, 8, 2, 2)
BATCH = ("y_lo", "x")
SEQ = ("z", "y_hi", "core")
ACROSS = ("y_lo", "x", "y_hi")
ALONG = ("z", "core")
PEERS = 16
COUNT = PEERS * PEERS * ROWS
TOP = 60000.0
F32 = jnp.float32
BF16 = jnp.bfloat16


def gelu(u):
    return 0.5 * u * (1.0 + lax.erf(u * 0.7071067811865476))


def wide(v):
    return jnp.concatenate([v[j : j + 1] for j in range(v.shape[0])], axis=1)


def combined(got_ref):
    rows = got_ref.shape[1] // 2
    got = got_ref[...]
    means = got[:, :rows]
    mean = jnp.sum(means, axis=0) * (1.0 / PEERS)
    spread = means - mean
    total = jnp.sum(got[:, rows:], axis=0) + (PEERS * ROWS) * jnp.sum(spread * spread, axis=0)
    return mean, total * (1.0 / COUNT)


def norm_terms(layer, got_ref, gain_ref, bias_ref):
    mean, variance = combined(got_ref)
    factor = gain_ref[layer : layer + 1] * lax.rsqrt(wide(variance) + EPS)
    return wide(mean), factor, bias_ref[layer : layer + 1]


def largest(v):
    return jnp.max(jnp.max(v, axis=0, keepdims=True), axis=1, keepdims=True)


def output_bound(stream_got_ref, gain_ref, bias_ref, point_ref):
    mean, variance = combined(stream_got_ref)
    root = 1.01 * COUNT**0.5
    stream = root * jnp.sqrt(largest(variance + mean * mean))
    gated = root * largest(jnp.abs(gain_ref[1:2])) + 1.01 * largest(jnp.abs(bias_ref[1:2]))
    weights = jnp.sum(jnp.abs(point_ref[1].astype(F32)), axis=0, keepdims=True)
    return stream + gated * largest(weights) + 1e-30


def fold(v):
    return jnp.sum(v.reshape(-1, 8, v.shape[-1]), axis=0)


def put_stats(out_ref, mean, squares):
    rows = out_ref.shape[1] // 2
    for j in range(rows):
        for base, v in ((0, mean), (rows, squares)):
            piece = v[:, 128 * j : 128 * (j + 1)].reshape(1, 1, 128)
            out_ref[:, base + j : base + j + 1, :] = jnp.broadcast_to(piece, (PEERS, 1, 128))


def row_slice(i, size):
    return pl.ds(pl.multiple_of(i * size, size), size)


def deviations(refs, mean, channels):
    squares = jnp.zeros((8, channels), F32)
    for ref in refs:

        def step(i, acc, ref=ref):
            d = ref[row_slice(i, 64), :].astype(F32) - mean
            return acc + fold(d * d)

        squares = lax.fori_loop(0, ref.shape[0] // 64, step, squares, unroll=4)
    return jnp.sum(squares, axis=0, keepdims=True)


def pack_edges(core, gated_ref, x_ref, facing_ref, outer_ref):
    put_edges(core, gated_ref, facing_ref.at[:, :MID], outer_ref.at[:, :MID])
    for last, edge_ref in ((1 - core, facing_ref), (core, outer_ref)):
        rows = pl.ds(pl.multiple_of(NEAR + last * (ROWS - FAR - NEAR), NEAR), NEAR)
        edge_ref[:NEAR, MID:] = x_ref[rows, :MID]
        edge_ref[NEAR:, MID:] = x_ref[rows, MID:]


def shifted(total, sums):
    if sums is None:
        pivot = jnp.sum(fold(total), axis=0, keepdims=True) * (1.0 / total.shape[0])
        zero = jnp.zeros((8, total.shape[1]), F32)
        sums = (pivot, zero, zero)
    pivot, first, second = sums
    d = total - pivot
    return pivot, first + fold(d), second + fold(d * d)


def put_shifted(stats_ref, sums):
    pivot, first, second = sums
    offset = jnp.sum(first, axis=0, keepdims=True) * (1.0 / ROWS)
    squares = jnp.sum(second, axis=0, keepdims=True) - ROWS * offset * offset
    put_stats(stats_ref, pivot + offset, jnp.maximum(squares, 0.0))


def input_stats(place_ref, x_ref, facing_ref, outer_ref, out_ref):
    put_edges(place_ref[0], x_ref, facing_ref, outer_ref)
    acc = jnp.zeros((8, CH), F32)
    for r in range(0, ROWS, 64):
        acc += fold(x_ref[r : r + 64, :].astype(F32))
    mean = jnp.sum(acc, axis=0, keepdims=True) * (1.0 / ROWS)
    squares = jnp.zeros((8, CH), F32)
    for r in range(0, ROWS, 64):
        d = x_ref[r : r + 64, :].astype(F32) - mean
        squares += fold(d * d)
    put_stats(out_ref, mean, jnp.sum(squares, axis=0, keepdims=True))


def activate(piece, first, count, terms, act_ref, offset, flag=None):
    mean, factor, bias = terms

    def step(i, carry):
        v = piece[pl.ds(pl.multiple_of(first + i * CHUNK, CHUNK), CHUNK), :].astype(F32)
        a = gelu((v - mean) * factor + bias)
        if flag is not None:
            a = jnp.where(flag > 0, a, 0.0)
        act_ref[pl.ds(pl.multiple_of(offset + i * CHUNK, CHUNK), CHUNK), :] = a.astype(BF16)
        return carry

    lax.fori_loop(0, count // CHUNK, step, 0)


def conv_tiles(dilation, size, terms, center_ref, weights, conv_ref, stats_ref, act_ref):
    mean, factor, bias = terms
    sums = None
    done = 0
    for end in range(size, ROWS + size, size):
        for r in range(end - size, end, CHUNK):
            v = center_ref[r : r + CHUNK, :].astype(F32)
            act_ref[dilation + r : dilation + r + CHUNK, :] = gelu((v - mean) * factor + bias).astype(BF16)
        ready = ROWS if end == ROWS else end - dilation
        while done + size <= ready:
            rows = [act_ref[done + k * dilation : done + k * dilation + size, :] for k in range(3)]
            total = jnp.dot(jnp.concatenate(rows, axis=1), weights, preferred_element_type=F32)
            conv_ref[done : done + size, :] = total
            sums = shifted(total, sums)
            done += size
    put_shifted(stats_ref, sums)


def first_conv(
    place_ref,
    got_ref,
    gain_ref,
    bias_ref,
    taps_ref,
    near_ref,
    center_ref,
    cross_ref,
    conv_ref,
    stats_ref,
    act_ref,
):
    terms = norm_terms(0, got_ref, gain_ref, bias_ref)
    core = place_ref[0]
    activate(near_ref, 0, NEAR, terms, act_ref, (1 - core) * (NEAR + ROWS))
    activate(cross_ref, 0, NEAR, terms, act_ref, core * (NEAR + ROWS), place_ref[1])
    weights = taps_ref[0].reshape(3 * CH, MID)
    conv_tiles(NEAR, 256, terms, center_ref, weights, conv_ref, stats_ref, act_ref)


def second_conv(
    place_ref,
    got_ref,
    gain_ref,
    bias_ref,
    taps_ref,
    point_ref,
    near_ref,
    near_packed_ref,
    center_ref,
    cross_ref,
    cross_packed_ref,
    conv_ref,
    stats_ref,
    act_ref,
    near_stream_ref,
    cross_stream_ref,
):
    terms = norm_terms(1, got_ref, gain_ref, bias_ref)
    core = place_ref[0]
    for side, x_ref, packed_ref, stream_ref in (
        (core, near_ref, near_packed_ref, near_stream_ref),
        (1 - core, cross_ref, cross_packed_ref, cross_stream_ref),
    ):
        stream_ref[...] = jnp.dot(packed_ref[:, :MID], point_ref[0], preferred_element_type=F32)
        close = pl.ds(pl.multiple_of(side * NEAR, NEAR), NEAR)
        distant = pl.ds(pl.multiple_of((1 - side) * NEAR, NEAR), NEAR)
        stream_ref[close, :] += x_ref[...].astype(F32)
        stream_ref[distant, :MID] += packed_ref[:NEAR, MID:].astype(F32)
        stream_ref[distant, MID:] += packed_ref[NEAR:, MID:].astype(F32)
    activate(near_stream_ref, 0, FAR, terms, act_ref, (1 - core) * (FAR + ROWS))
    activate(cross_stream_ref, 0, FAR, terms, act_ref, core * (FAR + ROWS), place_ref[1])
    weights = taps_ref[1].reshape(3 * CH, MID)
    conv_tiles(FAR, 512, terms, center_ref, weights, conv_ref, stats_ref, act_ref)


def put_edges(core, rows_ref, facing_ref, outer_ref):
    size = facing_ref.shape[0]
    last = ROWS - size
    facing_ref[...] = rows_ref[pl.ds(pl.multiple_of((1 - core) * last, 256), size), :]
    outer_ref[...] = rows_ref[pl.ds(pl.multiple_of(core * last, 256), size), :]


def gated_tile(conv_ref, i, terms, gated_ref):
    mean, factor, bias = terms
    for r in range(i * TILE, (i + 1) * TILE, CHUNK):
        gated_ref[r : r + CHUNK, :] = gelu((conv_ref[r : r + CHUNK, :] - mean) * factor + bias).astype(BF16)
    return gated_ref[i * TILE : (i + 1) * TILE, :]


def point_kernel(
    place_ref,
    got_ref,
    gain_ref,
    bias_ref,
    point_ref,
    conv_ref,
    x_ref,
    stream_ref,
    facing_ref,
    outer_ref,
    stats_ref,
    pool_ref,
    gated_ref,
):
    terms = norm_terms(0, got_ref, gain_ref, bias_ref)
    acc = jnp.zeros((8, CH), F32)
    bins = TILE // POOL
    for i in range(ROWS // TILE):
        rows = slice(i * TILE, (i + 1) * TILE)
        gated = gated_tile(conv_ref, i, terms, gated_ref)
        total = x_ref[rows, :].astype(F32) + jnp.dot(gated, point_ref[0], preferred_element_type=F32)
        stream_ref[rows, :] = total
        pool_ref[i * bins : (i + 1) * bins, :] = jnp.sum(total.reshape(bins, POOL, CH), axis=1)
        acc = acc + fold(total)
    pack_edges(place_ref[0], gated_ref, x_ref, facing_ref, outer_ref)
    mean = jnp.sum(acc, axis=0, keepdims=True) * (1.0 / ROWS)
    put_stats(stats_ref, mean, deviations((stream_ref,), mean, CH))


def pool_kernel(
    got_ref,
    stream_got_ref,
    gain_ref,
    bias_ref,
    point_ref,
    conv_ref,
    pool_ref,
    out_ref,
    bound_ref,
    gated_ref,
    sums_ref,
    flip_ref,
):
    bound = output_bound(stream_got_ref, gain_ref, bias_ref, point_ref)
    bound_ref[...] = jnp.broadcast_to(bound * (1.0 / TOP), bound_ref.shape)
    scale = (TOP / POOL) / bound
    terms = norm_terms(1, got_ref, gain_ref, bias_ref)
    bins = TILE // POOL
    row = lax.broadcasted_iota(jnp.int32, (bins, TILE), 0)
    col = lax.broadcasted_iota(jnp.int32, (bins, TILE), 1)
    pick = jnp.where(col // POOL == row, 1.0, 0.0).astype(BF16)

    for i in range(ROWS // TILE):
        gated = gated_tile(conv_ref, i, terms, gated_ref)
        sums_ref[i * bins : (i + 1) * bins, :] = jnp.dot(pick, gated, preferred_element_type=F32)
    sums = sums_ref[...]
    upper = sums.astype(BF16)
    lower = (sums - upper.astype(F32)).astype(BF16)
    branch = jnp.dot(upper, point_ref[1], preferred_element_type=F32)
    branch += jnp.dot(lower, point_ref[1], preferred_element_type=F32)
    flipped = ((pool_ref[...] + branch) * scale).T
    size = CH // HEADS
    for k in range(ROWS // POOL // 128):
        half = flip_ref.at[k]
        for h in range(HEADS):
            half[pl.ds(h, size, stride=HEADS), :] = flipped[h * size : (h + 1) * size, 128 * k : 128 * (k + 1)]
        out_ref[:, 128 * k : 128 * (k + 1)] = half[...]


VMEM = pl.BlockSpec(memory_space=pltpu.VMEM)
SMEM = pl.BlockSpec(memory_space=pltpu.SMEM)
PARAMS = pltpu.CompilerParams(vmem_limit_bytes=20 * 1024 * 1024)


def call(body, args, outs, scratch=(), scalars=0):
    return pl.pallas_call(
        body,
        out_shape=[jax.ShapeDtypeStruct(s, d) for s, d in outs],
        in_specs=[SMEM] * scalars + [VMEM] * (len(args) - scalars),
        out_specs=[VMEM] * len(outs),
        scratch_shapes=list(scratch),
        compiler_params=PARAMS,
    )(*args)


def halos(facing, outer):
    peers = lax.axis_size(SEQ)
    near = lax.ppermute(facing, SEQ, [(i, i ^ 1) for i in range(peers)])
    pairs = [(i, i + 1) for i in range(1, peers - 1, 2)]
    return near, lax.ppermute(outer, SEQ, pairs + [(j, i) for i, j in pairs])


def reduce_stats(sent, first, second, *edges):
    got = lax.all_to_all(sent, first, 0, 0, tiled=True)
    rows = got.shape[1] // 2
    means = got[:, :rows]
    mean = jnp.mean(means, axis=0)
    spread = means - mean
    squares = jnp.sum(got[:, rows:], axis=0) + ROWS * jnp.sum(spread * spread, axis=0)
    both = jnp.concatenate([mean, squares])
    if edges:
        both, *edges = lax.optimization_barrier((both, *edges))
        edges = halos(*edges)
    return lax.all_to_all(jnp.broadcast_to(both[None], sent.shape), second, 0, 0, tiled=True), *edges


def per_device(inputs, taps, point, in_gain, in_bias, mid_gain, mid_bias):
    place = lax.axis_index(SEQ)
    core = lax.axis_index("core")
    joined = jnp.where(core == 0, place > 0, place < lax.axis_size(SEQ) - 1)
    where = jnp.stack([core, joined.astype(core.dtype)]).astype(jnp.int32)
    x = inputs.reshape(ROWS, CH)
    wide_stats = ((PEERS, 8, 128), F32)
    slim_stats = ((PEERS, 4, 128), F32)
    conv_outs = [((ROWS, MID), F32), slim_stats]

    edge = ((NEAR, CH), BF16)
    facing, outer, stats = call(
        input_stats,
        (where, x),
        [edge, edge, wide_stats],
        scalars=1,
    )
    near, cross = halos(facing, outer)
    (got,) = reduce_stats(stats, ACROSS, ALONG)
    conv, stats = call(
        first_conv,
        (where, got, in_gain, in_bias, taps, near, x, cross),
        conv_outs,
        [pltpu.VMEM((ROWS + 2 * NEAR, CH), BF16)],
        1,
    )
    (got,) = reduce_stats(stats, ACROSS, ALONG)
    edge = ((FAR, CH), BF16)
    stream, facing, outer, stats, pooled = call(
        point_kernel,
        (where, got, mid_gain, mid_bias, point, conv, x),
        [((ROWS, CH), F32), edge, edge, wide_stats, ((ROWS // POOL, CH), F32)],
        [pltpu.VMEM((ROWS, MID), BF16)],
        1,
    )
    stream_got, near_packed, cross_packed = reduce_stats(stats, ACROSS, ALONG, facing, outer)
    conv, stats = call(
        second_conv,
        (where, stream_got, in_gain, in_bias, taps, point, near, near_packed, stream, cross, cross_packed),
        conv_outs,
        [
            pltpu.VMEM((ROWS + 2 * FAR, CH), BF16),
            pltpu.VMEM((FAR, CH), F32),
            pltpu.VMEM((FAR, CH), F32),
        ],
        1,
    )
    (got,) = reduce_stats(stats, ACROSS, ALONG)
    out, bound = call(
        pool_kernel,
        (got, stream_got, mid_gain, mid_bias, point, conv, pooled),
        [((CH, ROWS // POOL), F32), ((1, ROWS // POOL), F32)],
        [
            pltpu.VMEM((ROWS, MID), BF16),
            pltpu.VMEM((ROWS // POOL, MID), F32),
            pltpu.VMEM((ROWS // POOL // 128, CH, 128), F32),
        ],
    )
    bins = ROWS // POOL
    out = lax.all_to_all(out.reshape(CH // HEADS, HEADS, bins).astype(jnp.float16), SEQ, 0, 0, tiled=True)
    peers = lax.axis_size(SEQ)
    out = out.astype(F32).reshape(peers, -1, HEADS, bins) * bound.reshape(1, 1, 1, bins)
    return out.transpose(2, 1, 0, 3).reshape(1, HEADS, -1, peers * bins)


def solution(mesh):
    fine = Mesh(mesh.devices.reshape(SIZES), NAMES)
    return jax.shard_map(
        per_device,
        mesh=fine,
        in_specs=(P(BATCH, SEQ, None), P(), P(), P(), P(), P(), P()),
        out_specs=P(BATCH, None, SEQ, None),
        check_vma=False,
    )
```

```python
import jax
import jax.numpy as jnp
from jax import lax
from jax.experimental import pallas as pl
from jax.experimental.pallas import tpu as pltpu
from jax.sharding import Mesh, PartitionSpec as P

EPS = 1e-05
HEADS = 8
POOL = 8
ROWS = 2048
CH = 512
MID = 256
TILE = 256
CHUNK = 32
NEAR = 256
FAR = 512

NAMES = ("y_lo", "x", "z", "y_hi", "core")
SIZES = (2, 4, 8, 2, 2)
BATCH = ("y_lo", "x")
SEQ = ("z", "y_hi", "core")
ACROSS = ("y_lo", "x", "y_hi")
ALONG = ("z", "core")
PEERS = 16
COUNT = PEERS * PEERS * ROWS
TOP = 60000.0
F32 = jnp.float32
BF16 = jnp.bfloat16


def gelu(u):
    return 0.5 * u * (1.0 + lax.erf(u * 0.7071067811865476))


def wide(v):
    return jnp.concatenate([v[j : j + 1] for j in range(v.shape[0])], axis=1)


def combined(got_ref):
    rows = got_ref.shape[1] // 2
    got = got_ref[...]
    means = got[:, :rows]
    mean = jnp.sum(means, axis=0) * (1.0 / PEERS)
    spread = means - mean
    total = jnp.sum(got[:, rows:], axis=0) + (PEERS * ROWS) * jnp.sum(spread * spread, axis=0)
    return mean, total * (1.0 / COUNT)


def norm_terms(layer, got_ref, gain_ref, bias_ref):
    mean, variance = combined(got_ref)
    factor = gain_ref[layer : layer + 1] * lax.rsqrt(wide(variance) + EPS)
    return wide(mean), factor, bias_ref[layer : layer + 1]


def largest(v):
    return jnp.max(jnp.max(v, axis=0, keepdims=True), axis=1, keepdims=True)


def output_bound(stream_got_ref, gain_ref, bias_ref, point_ref):
    mean, variance = combined(stream_got_ref)
    root = 1.01 * COUNT**0.5
    stream = root * jnp.sqrt(largest(variance + mean * mean))
    gated = root * largest(jnp.abs(gain_ref[1:2])) + 1.01 * largest(jnp.abs(bias_ref[1:2]))
    weights = jnp.sum(jnp.abs(point_ref[1].astype(F32)), axis=0, keepdims=True)
    return stream + gated * largest(weights) + 1e-30


def fold(v):
    return jnp.sum(v.reshape(-1, 8, v.shape[-1]), axis=0)


def put_stats(out_ref, mean, squares):
    rows = out_ref.shape[1] // 2
    for j in range(rows):
        for base, v in ((0, mean), (rows, squares)):
            piece = v[:, 128 * j : 128 * (j + 1)].reshape(1, 1, 128)
            out_ref[:, base + j : base + j + 1, :] = jnp.broadcast_to(piece, (PEERS, 1, 128))


def row_slice(i, size):
    return pl.ds(pl.multiple_of(i * size, size), size)


def deviations(refs, mean, channels):
    squares = jnp.zeros((8, channels), F32)
    for ref in refs:

        def step(i, acc, ref=ref):
            d = ref[row_slice(i, 64), :].astype(F32) - mean
            return acc + fold(d * d)

        squares = lax.fori_loop(0, ref.shape[0] // 64, step, squares, unroll=4)
    return jnp.sum(squares, axis=0, keepdims=True)


def pack_edges(core, gated_ref, x_ref, facing_ref, outer_ref):
    put_edges(core, gated_ref, facing_ref.at[:, :MID], outer_ref.at[:, :MID])
    for last, edge_ref in ((1 - core, facing_ref), (core, outer_ref)):
        rows = pl.ds(pl.multiple_of(NEAR + last * (ROWS - FAR - NEAR), NEAR), NEAR)
        edge_ref[:NEAR, MID:] = x_ref[rows, :MID]
        edge_ref[NEAR:, MID:] = x_ref[rows, MID:]


def shifted(total, sums):
    if sums is None:
        pivot = jnp.sum(fold(total), axis=0, keepdims=True) * (1.0 / total.shape[0])
        zero = jnp.zeros((8, total.shape[1]), F32)
        sums = (pivot, zero, zero)
    pivot, first, second = sums
    d = total - pivot
    return pivot, first + fold(d), second + fold(d * d)


def put_shifted(stats_ref, sums):
    pivot, first, second = sums
    offset = jnp.sum(first, axis=0, keepdims=True) * (1.0 / ROWS)
    squares = jnp.sum(second, axis=0, keepdims=True) - ROWS * offset * offset
    put_stats(stats_ref, pivot + offset, jnp.maximum(squares, 0.0))


def input_stats(place_ref, x_ref, facing_ref, outer_ref, out_ref):
    put_edges(place_ref[0], x_ref, facing_ref, outer_ref)
    acc = jnp.zeros((8, CH), F32)
    for r in range(0, ROWS, 64):
        acc += fold(x_ref[r : r + 64, :].astype(F32))
    mean = jnp.sum(acc, axis=0, keepdims=True) * (1.0 / ROWS)
    squares = jnp.zeros((8, CH), F32)
    for r in range(0, ROWS, 64):
        d = x_ref[r : r + 64, :].astype(F32) - mean
        squares += fold(d * d)
    put_stats(out_ref, mean, jnp.sum(squares, axis=0, keepdims=True))


def activate(piece, first, count, terms, act_ref, offset, flag=None):
    mean, factor, bias = terms

    def step(i, carry):
        v = piece[pl.ds(pl.multiple_of(first + i * CHUNK, CHUNK), CHUNK), :].astype(F32)
        a = gelu((v - mean) * factor + bias)
        if flag is not None:
            a = jnp.where(flag > 0, a, 0.0)
        act_ref[pl.ds(pl.multiple_of(offset + i * CHUNK, CHUNK), CHUNK), :] = a.astype(BF16)
        return carry

    lax.fori_loop(0, count // CHUNK, step, 0)


def conv_tiles(dilation, size, terms, center_ref, weights, conv_ref, stats_ref, act_ref):
    mean, factor, bias = terms
    sums = None
    done = 0
    for end in range(size, ROWS + size, size):
        for r in range(end - size, end, CHUNK):
            v = center_ref[r : r + CHUNK, :].astype(F32)
            act_ref[dilation + r : dilation + r + CHUNK, :] = gelu((v - mean) * factor + bias).astype(BF16)
        ready = ROWS if end == ROWS else end - dilation
        while done + size <= ready:
            rows = [act_ref[done + k * dilation : done + k * dilation + size, :] for k in range(3)]
            total = jnp.dot(jnp.concatenate(rows, axis=1), weights, preferred_element_type=F32)
            conv_ref[done : done + size, :] = total
            sums = shifted(total, sums)
            done += size
    put_shifted(stats_ref, sums)


def first_conv(
    place_ref,
    got_ref,
    gain_ref,
    bias_ref,
    taps_ref,
    near_ref,
    center_ref,
    cross_ref,
    conv_ref,
    stats_ref,
    act_ref,
):
    terms = norm_terms(0, got_ref, gain_ref, bias_ref)
    core = place_ref[0]
    activate(near_ref, 0, NEAR, terms, act_ref, (1 - core) * (NEAR + ROWS))
    activate(cross_ref, 0, NEAR, terms, act_ref, core * (NEAR + ROWS), place_ref[1])
    weights = taps_ref[0].reshape(3 * CH, MID)
    conv_tiles(NEAR, 256, terms, center_ref, weights, conv_ref, stats_ref, act_ref)


def second_conv(
    place_ref,
    got_ref,
    gain_ref,
    bias_ref,
    taps_ref,
    point_ref,
    near_ref,
    near_packed_ref,
    center_ref,
    cross_ref,
    cross_packed_ref,
    conv_ref,
    stats_ref,
    act_ref,
    near_stream_ref,
    cross_stream_ref,
):
    terms = norm_terms(1, got_ref, gain_ref, bias_ref)
    core = place_ref[0]
    for side, x_ref, packed_ref, stream_ref in (
        (core, near_ref, near_packed_ref, near_stream_ref),
        (1 - core, cross_ref, cross_packed_ref, cross_stream_ref),
    ):
        stream_ref[...] = jnp.dot(packed_ref[:, :MID], point_ref[0], preferred_element_type=F32)
        close = pl.ds(pl.multiple_of(side * NEAR, NEAR), NEAR)
        distant = pl.ds(pl.multiple_of((1 - side) * NEAR, NEAR), NEAR)
        stream_ref[close, :] += x_ref[...].astype(F32)
        stream_ref[distant, :MID] += packed_ref[:NEAR, MID:].astype(F32)
        stream_ref[distant, MID:] += packed_ref[NEAR:, MID:].astype(F32)
    activate(near_stream_ref, 0, FAR, terms, act_ref, (1 - core) * (FAR + ROWS))
    activate(cross_stream_ref, 0, FAR, terms, act_ref, core * (FAR + ROWS), place_ref[1])
    weights = taps_ref[1].reshape(3 * CH, MID)
    conv_tiles(FAR, 512, terms, center_ref, weights, conv_ref, stats_ref, act_ref)


def put_edges(core, rows_ref, facing_ref, outer_ref):
    size = facing_ref.shape[0]
    last = ROWS - size
    facing_ref[...] = rows_ref[pl.ds(pl.multiple_of((1 - core) * last, 256), size), :]
    outer_ref[...] = rows_ref[pl.ds(pl.multiple_of(core * last, 256), size), :]


def gated_tile(conv_ref, i, terms, gated_ref):
    mean, factor, bias = terms
    for r in range(i * TILE, (i + 1) * TILE, CHUNK):
        gated_ref[r : r + CHUNK, :] = gelu((conv_ref[r : r + CHUNK, :] - mean) * factor + bias).astype(BF16)
    return gated_ref[i * TILE : (i + 1) * TILE, :]


def point_kernel(
    place_ref,
    got_ref,
    gain_ref,
    bias_ref,
    point_ref,
    conv_ref,
    x_ref,
    stream_ref,
    facing_ref,
    outer_ref,
    stats_ref,
    pool_ref,
    gated_ref,
):
    terms = norm_terms(0, got_ref, gain_ref, bias_ref)
    acc = jnp.zeros((8, CH), F32)
    bins = TILE // POOL
    for i in range(ROWS // TILE):
        rows = slice(i * TILE, (i + 1) * TILE)
        gated = gated_tile(conv_ref, i, terms, gated_ref)
        total = x_ref[rows, :].astype(F32) + jnp.dot(gated, point_ref[0], preferred_element_type=F32)
        stream_ref[rows, :] = total
        pool_ref[i * bins : (i + 1) * bins, :] = jnp.sum(total.reshape(bins, POOL, CH), axis=1)
        acc = acc + fold(total)
    pack_edges(place_ref[0], gated_ref, x_ref, facing_ref, outer_ref)
    mean = jnp.sum(acc, axis=0, keepdims=True) * (1.0 / ROWS)
    put_stats(stats_ref, mean, deviations((stream_ref,), mean, CH))


def pool_kernel(
    got_ref,
    stream_got_ref,
    gain_ref,
    bias_ref,
    point_ref,
    conv_ref,
    pool_ref,
    out_ref,
    bound_ref,
    gated_ref,
    sums_ref,
    flip_ref,
):
    bound = output_bound(stream_got_ref, gain_ref, bias_ref, point_ref)
    bound_ref[...] = jnp.broadcast_to(bound * (1.0 / TOP), bound_ref.shape)
    scale = (TOP / POOL) / bound
    terms = norm_terms(1, got_ref, gain_ref, bias_ref)
    bins = TILE // POOL
    row = lax.broadcasted_iota(jnp.int32, (bins, TILE), 0)
    col = lax.broadcasted_iota(jnp.int32, (bins, TILE), 1)
    pick = jnp.where(col // POOL == row, 1.0, 0.0).astype(BF16)

    for i in range(ROWS // TILE):
        gated = gated_tile(conv_ref, i, terms, gated_ref)
        sums_ref[i * bins : (i + 1) * bins, :] = jnp.dot(pick, gated, preferred_element_type=F32)
    sums = sums_ref[...]
    upper = sums.astype(BF16)
    lower = (sums - upper.astype(F32)).astype(BF16)
    branch = jnp.dot(upper, point_ref[1], preferred_element_type=F32)
    branch += jnp.dot(lower, point_ref[1], preferred_element_type=F32)
    flipped = ((pool_ref[...] + branch) * scale).T
    size = CH // HEADS
    for k in range(ROWS // POOL // 128):
        half = flip_ref.at[k]
        for h in range(HEADS):
            half[pl.ds(h, size, stride=HEADS), :] = flipped[h * size : (h + 1) * size, 128 * k : 128 * (k + 1)]
        out_ref[:, 128 * k : 128 * (k + 1)] = half[...]


VMEM = pl.BlockSpec(memory_space=pltpu.VMEM)
SMEM = pl.BlockSpec(memory_space=pltpu.SMEM)
PARAMS = pltpu.CompilerParams(vmem_limit_bytes=20 * 1024 * 1024)


def call(body, args, outs, scratch=(), scalars=0):
    return pl.pallas_call(
        body,
        out_shape=[jax.ShapeDtypeStruct(s, d) for s, d in outs],
        in_specs=[SMEM] * scalars + [VMEM] * (len(args) - scalars),
        out_specs=[VMEM] * len(outs),
        scratch_shapes=list(scratch),
        compiler_params=PARAMS,
    )(*args)


def halos(facing, outer):
    peers = lax.axis_size(SEQ)
    near = lax.ppermute(facing, SEQ, [(i, i ^ 1) for i in range(peers)])
    pairs = [(i, i + 1) for i in range(1, peers - 1, 2)]
    return near, lax.ppermute(outer, SEQ, pairs + [(j, i) for i, j in pairs])


def reduce_stats(sent, first, second, *edges):
    got = lax.all_to_all(sent, first, 0, 0, tiled=True)
    rows = got.shape[1] // 2
    means = got[:, :rows]
    mean = jnp.mean(means, axis=0)
    spread = means - mean
    squares = jnp.sum(got[:, rows:], axis=0) + ROWS * jnp.sum(spread * spread, axis=0)
    both = jnp.concatenate([mean, squares])
    if edges:
        both, *edges = lax.optimization_barrier((both, *edges))
        edges = halos(*edges)
    return lax.all_to_all(jnp.broadcast_to(both[None], sent.shape), second, 0, 0, tiled=True), *edges


def per_device(inputs, taps, point, in_gain, in_bias, mid_gain, mid_bias):
    place = lax.axis_index(SEQ)
    core = lax.axis_index("core")
    joined = jnp.where(core == 0, place > 0, place < lax.axis_size(SEQ) - 1)
    where = jnp.stack([core, joined.astype(core.dtype)]).astype(jnp.int32)
    x = inputs.reshape(ROWS, CH)
    wide_stats = ((PEERS, 8, 128), F32)
    slim_stats = ((PEERS, 4, 128), F32)
    conv_outs = [((ROWS, MID), F32), slim_stats]

    edge = ((NEAR, CH), BF16)
    facing, outer, stats = call(
        input_stats,
        (where, x),
        [edge, edge, wide_stats],
        scalars=1,
    )
    near, cross = halos(facing, outer)
    (got,) = reduce_stats(stats, ACROSS, ALONG)
    conv, stats = call(
        first_conv,
        (where, got, in_gain, in_bias, taps, near, x, cross),
        conv_outs,
        [pltpu.VMEM((ROWS + 2 * NEAR, CH), BF16)],
        1,
    )
    (got,) = reduce_stats(stats, ACROSS, ALONG)
    edge = ((FAR, CH), BF16)
    stream, facing, outer, stats, pooled = call(
        point_kernel,
        (where, got, mid_gain, mid_bias, point, conv, x),
        [((ROWS, CH), F32), edge, edge, wide_stats, ((ROWS // POOL, CH), F32)],
        [pltpu.VMEM((ROWS, MID), BF16)],
        1,
    )
    stream_got, near_packed, cross_packed = reduce_stats(stats, ACROSS, ALONG, facing, outer)
    conv, stats = call(
        second_conv,
        (where, stream_got, in_gain, in_bias, taps, point, near, near_packed, stream, cross, cross_packed),
        conv_outs,
        [
            pltpu.VMEM((ROWS + 2 * FAR, CH), BF16),
            pltpu.VMEM((FAR, CH), F32),
            pltpu.VMEM((FAR, CH), F32),
        ],
        1,
    )
    (got,) = reduce_stats(stats, ALONG, ACROSS)
    out, bound = call(
        pool_kernel,
        (got, stream_got, mid_gain, mid_bias, point, conv, pooled),
        [((CH, ROWS // POOL), F32), ((1, ROWS // POOL), F32)],
        [
            pltpu.VMEM((ROWS, MID), BF16),
            pltpu.VMEM((ROWS // POOL, MID), F32),
            pltpu.VMEM((ROWS // POOL // 128, CH, 128), F32),
        ],
    )
    bins = ROWS // POOL
    out = lax.all_to_all(out.reshape(CH // HEADS, HEADS, bins).astype(jnp.float16), SEQ, 0, 0, tiled=True)
    peers = lax.axis_size(SEQ)
    out = out.astype(F32).reshape(peers, -1, HEADS, bins) * bound.reshape(1, 1, 1, bins)
    return out.transpose(2, 1, 0, 3).reshape(1, HEADS, -1, peers * bins)


def solution(mesh):
    fine = Mesh(mesh.devices.reshape(SIZES), NAMES)
    return jax.shard_map(
        per_device,
        mesh=fine,
        in_specs=(P(BATCH, SEQ, None), P(), P(), P(), P(), P(), P()),
        out_specs=P(BATCH, None, SEQ, None),
        check_vma=False,
    )
```
